256 devices in a mesh: ex: 8 (over x_lo, y), wa: 32 (over z, x_hi, core).
Axes of the slice: x: 4 (x_hi: 2, x_lo: 2; x = x_hi * 2 + x_lo), y: 4, z: 8, core: 2. Of those that a mesh axis runs over, the one named last changes fastest.
Arguments:
- gradients: bfloat16 [2560, 163840], P('ex', 'wa'), may hold values from -0.109375 to 0.109375
- coeffs: float32 [2560], P('ex'), may hold values from 0.3 to 3
Outputs:
- influence: float32 [2560, 2560], P('ex', 'wa')
The draws below stay inside these ranges and needn't reach their ends.
All inputs are finite; a program needn't handle non-finite values.
Results may differ from the reference program's by a relative error of at most 0.0005.
Values may be sent and summed in bfloat16 or wider, within the bound.
No kernel may reach another device: no remote copies, remote signals or barrier semaphores. Data moves between devices by JAX's collectives and lax.ppermute only.
A program may use at most 128 MiB of HBM per device.

```python
import math
import jax
import jax.numpy as jnp

GW = 163840
NEX = 2560


def spiked(drawn, own_key, source, target, shards_of, factor):
    def block_of(dim):
        return (jnp.arange(drawn.shape[dim]) // (drawn.shape[dim] // shards_of)).reshape((-1,) + (1,) * (drawn.ndim - 1 - dim))

    one_side = jax.random.permutation(own_key, shards_of)[block_of(target)]
    far = (block_of(target) + shards_of // 2) % shards_of
    return jnp.where((block_of(source) == one_side) | (block_of(source) == far), factor * drawn, drawn)


def steps_of(own_key, extent, split, smallest, top_value):
    factor_of, own = 1.0, jax.random.fold_in(own_key, 6)
    for dim, blocks in split:
        steps = jnp.exp(jax.random.uniform(jax.random.fold_in(own, dim), (blocks,), jnp.float32, smallest / len(split), top_value / len(split)))
        factor_of = factor_of * jnp.repeat(steps, extent[dim] // blocks).reshape([-1 if axis == dim else 1 for axis in range(len(extent))])
    return factor_of


def bell_draw_with(own_key, shape, deviation, most, cuts, heavy, held_as=jnp.bfloat16):
    array = deviation * jax.random.normal(own_key, shape, jnp.float32)
    if cuts:
        array = array * steps_of(own_key, shape, cuts, -0.22, 0.18)
    return jnp.clip(spiked(array, jax.random.fold_in(own_key, 3), *heavy), -most, most).astype(held_as)


def setup_inputs(seed: int = 0) -> dict:
    streams_of = jax.random.split(jax.random.key(seed), 3)
    gradients = bell_draw_with(streams_of[0], (NEX, GW), (GW // 16) ** -0.5, 0.109375, ((0, 8), (1, 32)), (1, 0, 32, 2.75))
    coeffs = jnp.clip(jnp.exp(math.log(3.0) - 2.3025851 * jax.random.uniform(streams_of[1], (NEX,), jnp.float32) ** steps_of(streams_of[1], (NEX,), ((0, 8),), -0.2, 0.2)), 0.3, 3.0)
    return {"gradients": gradients, "coeffs": coeffs}


def reference(gradients, coeffs):
    gram = jnp.dot(gradients, gradients.T, preferred_element_type=jnp.float32)
    return (coeffs[:, None] * gram) * coeffs[None, :]
```

```python
import jax
import jax.numpy as jnp
from jax import lax
from jax.sharding import PartitionSpec as P

NB = 8
NK = 5


def moved(value, route):
    pairs = []
    for e in range(NB):
        for w in range(4 * NB):
            to = route(e, w // 4, w // 2 % 2, w % 2)
            if to is not None:
                te, tz, th, tc = to
                pairs.append((e * 4 * NB + w, te * 4 * NB + tz * 4 + th * 2 + tc))
    return lax.ppermute(value, ("ex", "wa"), pairs)


def dots(left, right):
    return lax.dot_general(
        left, right, (((1,), (1,)), ((), ())), preferred_element_type=jnp.float32
    )


def per_device(gradients, coeffs):
    rows, width = gradients.shape
    quarter = rows // 4
    e = lax.axis_index("ex")
    w = lax.axis_index("wa")
    z, h, c = w // 4, w // 2 % 2, w % 2

    most = jnp.max(jnp.abs(gradients)).astype(jnp.float32)
    info = jnp.concatenate([coeffs, jnp.zeros((1024 - 128 - rows,), jnp.float32), jnp.full((128,), most)])
    every = lax.all_gather(info.reshape(8, 128), ("ex", "wa"), axis=0, tiled=False)
    most = jnp.max(every[:, 7, :])
    column_coeffs = lax.dynamic_index_in_dim(every, z * 4 * NB, 0, keepdims=False).reshape(1024)[:rows]
    column_coeffs = lax.dynamic_slice_in_dim(column_coeffs, (w % 4) * quarter, quarter)
    bound = jnp.maximum(most * most * (2 * width // NB), 1e-30)
    scale, back = 4096.0 / bound, bound * (1.0 / 4096.0)

    mine = lax.all_to_all(gradients.reshape(rows, NB, width // NB), "ex", 1, 0)
    other = moved(mine, lambda e, z, h, c: (e, z, h, 1 - c))

    def cores_rows(block):
        own = lax.dynamic_index_in_dim(block.reshape(NB, 2, 2, quarter, -1), c, 2, keepdims=False)
        own = own.reshape(NB, 2 * quarter, -1)
        return jnp.concatenate([own, own[: NK - 1]], 0)

    right0, right1 = cores_rows(mine), cores_rows(other)
    parts = []
    for i in range(NB):
        k = width // NB
        tile = dots(mine[i], right0[i : i + NK].reshape(-1, k)) + dots(other[i], right1[i : i + NK].reshape(-1, k))
        parts.append((tile * scale).astype(jnp.float16))
    parts = jnp.stack(parts)
    parts = lax.all_to_all(parts, "ex", 0, 0)
    summed = jnp.sum(parts.astype(jnp.float32), 0).astype(jnp.float16)

    eighth = rows // 8
    summed = summed.reshape(8, eighth, NK, 2, quarter).transpose(2, 3, 1, 0, 4).reshape(NK, 2, eighth, 8 * quarter)
    summed = jnp.concatenate([summed, jnp.zeros((NB - NK,) + summed.shape[1:], summed.dtype)], 0)
    summed = lax.dynamic_slice_in_dim(jnp.concatenate([summed, summed], 0), (NB - e) % NB, NB, 0)
    summed = summed.reshape(2 * NB, eighth, 8 * quarter)
    groups = [[zz * 4 + hh * 2 + cc for zz in range(NB) for hh in range(2)] for cc in range(2)]
    final = lax.all_to_all(summed, "wa", 0, 0, axis_index_groups=groups)
    final = jnp.sum(final.astype(jnp.float32), 0)
    final = final.reshape(eighth, 8, quarter).transpose(1, 0, 2).reshape(4, quarter, quarter) * back

    mirrored = jnp.zeros_like(final)
    for dh in range(2):
        for dc in range(2):
            piece = lax.dynamic_index_in_dim(final, (h ^ dh) * 2 + (c ^ dc), 0, keepdims=False).T
            route = lambda e, z, h, c: (z, e, h ^ dh, c ^ dc) if (z - e) % NB in (1, 2, 3) else None
            piece = moved(piece, route)
            mirrored = lax.dynamic_update_slice(
                mirrored, piece[None], ((h ^ dh) * 2 + (c ^ dc), jnp.int32(0), jnp.int32(0))
            )
    final = jnp.where((z - e) % NB < NK, final, mirrored).reshape(rows, quarter)
    return (coeffs[:, None] * final) * column_coeffs[None, :]


def solution(mesh):
    placed = (P("ex", "wa"), P("ex"))
    return jax.shard_map(
        per_device, mesh=mesh, in_specs=placed, out_specs=P("ex", "wa"), check_vma=False
    )
```

```python
import jax
import jax.numpy as jnp
from jax import lax
from jax.experimental import pallas as pl
from jax.experimental.pallas import tpu as pltpu
from jax.sharding import PartitionSpec as P

NB = 8


def moved(value, route):
    pairs = []
    for e in range(NB):
        for w in range(4 * NB):
            to = route(e, w // 4, w // 2 % 2, w % 2)
            if to is not None:
                te, tz, th, tc = to
                pairs.append((e * 4 * NB + w, te * 4 * NB + tz * 4 + th * 2 + tc))
    return lax.ppermute(value, ("ex", "wa"), pairs)


def dot_nt(left, right):
    return lax.dot_general(
        left, right, (((1,), (1,)), ((), ())), preferred_element_type=jnp.float32
    )


def products_kernel(core_ref, mine_ref, other_ref, out_ref, columns, block):
    i = pl.program_id(0)
    rows, k = mine_ref.shape[1:]
    quarter, half = rows // 4, rows // 2
    small = quarter // 2

    @pl.when(i == 0)
    def _():
        for j in range(NB + 4):
            for h in range(2):
                at = pl.ds(pl.multiple_of(h * half + core_ref[0] * quarter, quarter), quarter)
                to = pl.ds(j * half + h * quarter, quarter)
                columns[to, :k] = mine_ref[j % NB, at, :]
                columns[to, k:] = other_ref[j % NB, at, :]

    block[:, :k] = mine_ref[i]
    block[:, k:] = other_ref[i]
    start = pl.multiple_of(i * half, half)
    for piece in range(4):
        tile = dot_nt(columns[pl.ds(start + piece * half, half), :], block[...])
        for h in range(2):
            at = (2 * piece + h) * small
            out_ref[0, at : at + small, :rows] = tile[h * quarter : h * quarter + small]
            out_ref[0, at : at + small, rows:] = tile[h * quarter + small : (h + 1) * quarter]

    @pl.when(i < 4)
    def _():
        tile = dot_nt(columns[pl.ds(start + 4 * half, quarter), :], block[...])
        out_ref[0, 8 * small :, :rows] = tile[:small]
        out_ref[0, 8 * small :, rows:] = tile[small:]

    @pl.when(i >= 4)
    def _():
        tile = dot_nt(columns[pl.ds(start + 4 * half, half), :], block[half:, :])
        for q in range(4):
            out_ref[0, 8 * small :, q * half : (q + 1) * half] = tile[q * small : (q + 1) * small]


def products(core, mine, other):
    _, rows, k = mine.shape
    whole = pl.BlockSpec(mine.shape, lambda i: (0, 0, 0), memory_space=pltpu.VMEM)
    out_rows = 9 * rows // 8
    return pl.pallas_call(
        products_kernel,
        grid=(NB,),
        in_specs=[pl.BlockSpec(memory_space=pltpu.SMEM), whole, whole],
        out_specs=pl.BlockSpec((1, out_rows, 2 * rows), lambda i: (i, 0, 0)),
        out_shape=jax.ShapeDtypeStruct((NB, out_rows, 2 * rows), jnp.float32),
        scratch_shapes=[
            pltpu.VMEM((12 * rows // 2, 2 * k), jnp.bfloat16),
            pltpu.VMEM((rows, 2 * k), jnp.bfloat16),
        ],
        compiler_params=pltpu.CompilerParams(vmem_limit_bytes=40 * 1024 * 1024),
        cost_estimate=pl.CostEstimate(
            flops=2 * NB * 9 * rows // 4 * rows * 2 * k, bytes_accessed=NB * rows * (k * 4 + 9 * rows), transcendentals=0
        ),
    )(core, mine, other)


def per_device(gradients, coeffs):
    rows, width = gradients.shape
    quarter, small = rows // 4, rows // 8
    e = lax.axis_index("ex")
    w = lax.axis_index("wa")
    z, h, c = w // 4, w // 2 % 2, w % 2

    mine = jnp.stack([gradients[:, i * (width // NB) : (i + 1) * (width // NB)] for i in range(NB)])
    mine = lax.all_to_all(mine, "ex", 0, 0)
    other = moved(mine, lambda e, z, h, c: (e, z, h, 1 - c))
    column_coeffs = moved(coeffs, lambda e, z, h, c: (z, e, h, c))
    column_coeffs = lax.dynamic_slice_in_dim(column_coeffs, (w % 4) * quarter, quarter)

    most = jnp.broadcast_to(jnp.max(jnp.abs(gradients)).astype(jnp.float32), (8, 128))
    for piece in [moved(most, lambda e, z, h, c: ((e + d) % NB, z, h, c)) for d in range(1, NB)]:
        most = jnp.maximum(most, piece)
    most = jnp.maximum(most, moved(most, lambda e, z, h, c: (e, z, h, 1 - c)))
    all_most = jnp.maximum(most, moved(most, lambda e, z, h, c: (e, z, 1 - h, c)))
    for step in (1, 2, 4):
        all_most = jnp.maximum(all_most, moved(all_most, lambda e, z, h, c: (e, z ^ step, h, c)))

    def bound_of(most):
        return jnp.maximum(most[0, 0] * most[0, 0] * (2 * width // NB), 1e-30)

    bound, all_bound = bound_of(most), bound_of(all_most)

    parts = products(jnp.reshape(c, (1,)).astype(jnp.int32), mine, other)
    parts = (parts * (4096.0 / bound)).astype(jnp.float16)
    parts = lax.all_to_all(parts, "ex", 0, 0)
    summed = jnp.sum(parts.astype(jnp.float32), 0)
    summed = (summed * (bound / all_bound)).astype(jnp.float16).reshape(9, small, 2 * rows)

    blank = jnp.zeros((small, rows), summed.dtype)
    last = jnp.where(
        e < 4,
        jnp.stack([summed[8], jnp.zeros_like(summed[8])]),
        jnp.stack([jnp.concatenate([summed[8, :, :rows], blank], 1), jnp.concatenate([summed[8, :, rows:], blank], 1)]),
    )
    blanks = jnp.zeros((6, small, 2 * rows), summed.dtype)
    summed = jnp.concatenate([summed[:8], last, blanks], 0)
    summed = lax.dynamic_slice_in_dim(jnp.concatenate([summed, summed], 0), (NB - e) % NB * 2, 2 * NB, 0)
    groups = [[zz * 4 + hh * 2 + cc for zz in range(NB) for hh in range(2)] for cc in range(2)]
    final = lax.all_to_all(summed, "wa", 0, 0, axis_index_groups=groups)
    final = jnp.sum(final.astype(jnp.float32), 0) * (all_bound * (1.0 / 4096.0))

    normal = jnp.concatenate([final[:, :rows], final[:, rows:]], 0)
    lower = jnp.concatenate([final[:, : rows // 2], final[:, rows // 2 : rows]], 0)
    lower = jnp.concatenate([jnp.zeros_like(lower), lower], 1)
    k = (z - e) % NB
    opposite = k == 4
    late = opposite & (e >= 4)
    final = jnp.where(late, lower, normal).reshape(quarter, 4, quarter).transpose(1, 0, 2)

    def mirror_route(dh, dc):
        def route(e, z, h, c):
            k = (z - e) % NB
            sends = k in (1, 2, 3) or (k == 4 and (h == 0 if e < 4 else h ^ dh == 1))
            return (z, e, h ^ dh, c ^ dc) if sends else None

        return route

    mirrored = jnp.zeros_like(final)
    for dh in range(2):
        for dc in range(2):
            there = (h ^ dh) * 2 + (c ^ dc)
            piece = lax.dynamic_index_in_dim(final, there, 0, keepdims=False)
            piece = moved(piece, mirror_route(dh, dc))
            mirrored = lax.dynamic_update_slice(mirrored, piece[None], (there, jnp.int32(0), jnp.int32(0)))
    upper_rows = jnp.arange(4)[:, None, None] < 2
    direct = (k < 4) | (opposite & jnp.where(e < 4, h == 0, ~upper_rows))
    final = jnp.where(direct, final.transpose(0, 2, 1), mirrored).reshape(rows, quarter)
    return (coeffs[:, None] * final) * column_coeffs[None, :]


def solution(mesh):
    placed = (P("ex", "wa"), P("ex"))
    return jax.shard_map(
        per_device, mesh=mesh, in_specs=placed, out_specs=P("ex", "wa"), check_vma=False
    )
```

```python
import jax
import jax.numpy as jnp
from jax import lax
from jax.experimental import pallas as pl
from jax.experimental.pallas import tpu as pltpu
from jax.sharding import PartitionSpec as P

NB = 8
LANES = 128
FIRST, SECOND, LAST = 960, 640, 200
TAIL = 8


def moved(value, route):
    pairs = []
    for e in range(NB):
        for w in range(4 * NB):
            to = route(e // 4, e % 4, w // 4, w // 2 % 2, w % 2)
            if to is not None:
                tx, ty, tz, th, tc = to
                pairs.append(((e * 4 * NB) + w, (tx * 4 + ty) * 4 * NB + tz * 4 + th * 2 + tc))
    return lax.ppermute(value, ("ex", "wa"), pairs)


def along_y(value, d):
    return moved(value, lambda x, y, z, h, c: (x, (y + d) % 4, z, h, c))


def along_x(value):
    return moved(value, lambda x, y, z, h, c: (1 - x, y, z, h, c))


def dot_nt(left, right):
    return lax.dot_general(
        left, right, (((1,), (1,)), ((), ())), preferred_element_type=jnp.float32
    )


def power_of_two(n):
    left, size = jnp.abs(n), jnp.ones_like(n)
    for bit in (64.0, 32.0, 16.0, 8.0, 4.0, 2.0, 1.0):
        has = left >= bit
        size = jnp.where(has, size * 2.0**bit, size)
        left = jnp.where(has, left - bit, left)
    return jnp.where(n < 0, 1.0 / size, size)


def products_kernel(core_ref, mine_ref, other_ref, first_ref, second_ref, columns, block, scale, exponent):
    i = pl.program_id(0)
    rows, k = mine_ref.shape[1:]
    quarter, half = rows // 4, rows // 2

    @pl.when(i == 0)
    def _():
        most = jnp.abs(mine_ref[0])
        for j in range(NB):
            most = jnp.maximum(most, jnp.maximum(jnp.abs(mine_ref[j]), jnp.abs(other_ref[j])))
            for h in range(2):
                at = pl.ds(pl.multiple_of(h * half + core_ref[0] * quarter, quarter), quarter)
                a, b = mine_ref[j, at, :], other_ref[j, at, :]
                for copy in (j, j + NB) if j < 4 else (j,):
                    to = pl.ds(copy * half + h * quarter, quarter)
                    columns[to, :k] = a
                    columns[to, k:] = b
        most = jnp.full((TAIL, LANES), jnp.max(most.astype(jnp.float32)))
        bound = jnp.maximum(most * most * (2.0 * k), 1e-30)
        n = jnp.ceil(jnp.log2(bound)) - 11.0
        exponent[...] = n
        scale[...] = power_of_two(-n)

    block[:, :k] = mine_ref[i]
    block[:, k:] = other_ref[i]
    start = pl.multiple_of(i * half, half)
    factor = scale[0:1, :]
    tile = dot_nt(block[...], columns[pl.ds(start, 4 * half), :])
    for t in range(3):
        first_ref[0, t * rows : (t + 1) * rows, :] = tile[:, t * LANES : (t + 1) * LANES] * factor
    for t in range(2):
        second_ref[0, t * rows : (t + 1) * rows, :] = tile[:, (t + 3) * LANES : (t + 4) * LANES] * factor
    first_ref[0, FIRST:, :] = exponent[...]
    second_ref[0, SECOND + LAST :, :] = exponent[...]

    @pl.when(i < 4)
    def _():
        tile = dot_nt(columns[pl.ds(start + 4 * half, quarter), :], block[...])
        second_ref[0, SECOND : SECOND + 80, :] = tile[:, :128] * factor
        second_ref[0, SECOND + 80 : SECOND + 160, :] = tile[:, 128:256] * factor
        second_ref[0, SECOND + 160 : SECOND + 200, :64] = tile[:40, 256:] * factor[:, :64]
        second_ref[0, SECOND + 160 : SECOND + 200, 64:] = tile[40:, 256:] * factor[:, :64]

    @pl.when(i >= 4)
    def _():
        tile = dot_nt(columns[pl.ds(start + 4 * half, half), :], block[half:, :])
        second_ref[0, SECOND : SECOND + 160, :] = tile[:, :128] * factor
        for q in range(4):
            second_ref[0, SECOND + 160 : SECOND + 200, q * 32 : (q + 1) * 32] = (
                tile[q * 40 : (q + 1) * 40, 128:] * factor[:, :32]
            )


def products(core, mine, other):
    _, rows, k = mine.shape
    whole = pl.BlockSpec(mine.shape, lambda i: (0, 0, 0))
    shapes = [(NB, FIRST + TAIL, LANES), (NB, SECOND + LAST + TAIL, LANES)]
    return pl.pallas_call(
        products_kernel,
        grid=(NB,),
        in_specs=[pl.BlockSpec(memory_space=pltpu.SMEM), whole, whole],
        out_specs=[pl.BlockSpec((1,) + s[1:], lambda i: (i, 0, 0)) for s in shapes],
        out_shape=[jax.ShapeDtypeStruct(s, jnp.float32) for s in shapes],
        scratch_shapes=[
            pltpu.VMEM((12 * rows // 2, 2 * k), jnp.bfloat16),
            pltpu.VMEM((rows, 2 * k), jnp.bfloat16),
            pltpu.VMEM((TAIL, LANES), jnp.float32),
            pltpu.VMEM((TAIL, LANES), jnp.float32),
        ],
        compiler_params=pltpu.CompilerParams(vmem_limit_bytes=40 * 1024 * 1024),
        cost_estimate=pl.CostEstimate(
            flops=2 * NB * 9 * rows // 4 * rows * 2 * k, bytes_accessed=NB * rows * (k * 4 + 9 * rows), transcendentals=0
        ),
    )(core, mine, other)


def pieces_kernel(first_ref, second_ref, out_ref):
    rows = FIRST // 3
    tile = jnp.concatenate(
        [first_ref[t * rows : (t + 1) * rows, :].T for t in range(3)]
        + [second_ref[t * rows : (t + 1) * rows, :].T for t in range(2)],
        axis=0,
    )
    for p in range(8):
        piece = tile[p * 80 : (p + 1) * 80]
        out_ref[p, 0:80, :] = piece[:, :128]
        out_ref[p, 80:160, :] = piece[:, 128:256]
        out_ref[p, 160:200, :64] = piece[:40, 256:]
        out_ref[p, 160:200, 64:] = piece[40:, 256:]
    out_ref[8] = second_ref[SECOND : SECOND + LAST, :]


def pieces_of(first, second):
    return pl.pallas_call(
        pieces_kernel,
        out_shape=jax.ShapeDtypeStruct((9, LAST, LANES), jnp.float32),
        cost_estimate=pl.CostEstimate(flops=0, bytes_accessed=1_843_200, transcendentals=0),
    )(first, second)


def split_scale(array):
    values = array[..., :-TAIL, :]
    return values, array.reshape(-1, LANES)[-1, 0].astype(jnp.float32)


def total_of(arrays, room):
    halves = [split_scale(a) for a in arrays]
    n = halves[0][1]
    for _, other in halves[1:]:
        n = jnp.maximum(n, other)
    n = n + room
    return sum(v.astype(jnp.float32) * power_of_two(m - n) for v, m in halves), n


def with_scale(values, n, dtype=jnp.float16):
    tail = jnp.broadcast_to(n.astype(dtype), values.shape[:-2] + (TAIL, LANES))
    return jnp.concatenate([values.astype(dtype), tail], axis=-2)


def per_device(gradients, coeffs):
    rows, width = gradients.shape
    quarter = rows // 4
    e = lax.axis_index("ex")
    w = lax.axis_index("wa")
    x, y = e // 4, e % 4
    z, h, c = w // 4, w // 2 % 2, w % 2

    mine = lax.all_to_all(gradients.reshape(rows, NB, width // NB), "ex", 1, 0)
    other = moved(mine, lambda x, y, z, h, c: (x, y, z, h, 1 - c))
    column_coeffs = moved(coeffs, lambda x, y, z, h, c: (z // 4, z % 4, 4 * x + y, h, c))
    column_coeffs = lax.dynamic_slice_in_dim(column_coeffs, (w % 4) * quarter, quarter)

    first, second = products(jnp.reshape(c, (1,)).astype(jnp.int32), mine, other)

    first = first.reshape(2, 4, FIRST + TAIL, LANES)
    second = second.reshape(2, 4, SECOND + LAST + TAIL, LANES)

    def at(array, index, axis):
        return lax.dynamic_index_in_dim(array, index, axis, keepdims=False)

    second_there = along_x(at(second, 1 - x, 0).astype(jnp.float16))
    first_there = [along_y(at(first, (y + d) % 4, 1).astype(jnp.float16), d) for d in (2, 1, 3)]
    second, n_second = total_of([at(second, x, 0), second_there], 1)
    first, n_first = total_of([at(first, y, 1)] + first_there, 2)

    second_there = [along_y(with_scale(at(second, (y + d) % 4, 0), n_second), d) for d in (2, 1, 3)]
    first_there = along_x(with_scale(at(first, 1 - x, 0), n_first))
    second, n_second = total_of([with_scale(at(second, y, 0), n_second, jnp.float32)] + second_there, 2)
    first, n_first = total_of([with_scale(at(first, x, 0), n_first, jnp.float32), first_there], 1)
    n = jnp.maximum(n_first, n_second)
    pieces = pieces_of(first * power_of_two(n_first - n), second * power_of_two(n_second - n))

    pieces = with_scale(pieces, n)
    blanks = jnp.zeros((6,) + pieces.shape[1:], pieces.dtype)
    pieces = jnp.concatenate([pieces, pieces[8:], blanks], 0)
    pieces = lax.dynamic_slice_in_dim(jnp.concatenate([pieces, pieces], 0), (NB - e) % NB * 2, 2 * NB, 0)
    groups = [[zz * 4 + hh * 2 + cc for zz in range(NB) for hh in range(2)] for cc in range(2)]
    parts = lax.all_to_all(pieces, "wa", 0, 0, axis_index_groups=groups)
    factors = power_of_two(parts[:, -1:, :1].astype(jnp.float32))
    final = jnp.sum(parts[:, :-TAIL].astype(jnp.float32) * factors, 0)

    normal = jnp.concatenate(
        [final[:80], final[80:160], jnp.concatenate([final[160:, :64], final[160:, 64:]], 0)], 1
    )
    rest = jnp.where(h == 0, final[160:, :64], final[160:, 64:])
    lower = jnp.concatenate(
        [jnp.where(h == 0, final[:80], final[80:160]), jnp.concatenate([rest[:, :32], rest[:, 32:]], 0)], 1
    )
    lower = jnp.concatenate([jnp.zeros_like(lower), lower], 1)
    k = (z - e) % NB
    opposite = k == 4
    final = jnp.where(opposite & (e >= 4), lower, normal).reshape(quarter, 4, quarter).transpose(1, 0, 2)

    def mirror_route(dh, dc):
        def route(x, y, z, h, c):
            e, k = 4 * x + y, (z - 4 * x - y) % NB
            sends = k in (1, 2, 3) or (k == 4 and (h == 0 if e < 4 else h ^ dh == 1))
            return (z // 4, z % 4, e, h ^ dh, c ^ dc) if sends else None

        return route

    def from_own(quarters):
        quarters = jnp.where(c == 1, jnp.stack([quarters[1], quarters[0], quarters[3], quarters[2]]), quarters)
        return jnp.where(h == 1, jnp.stack([quarters[2], quarters[3], quarters[0], quarters[1]]), quarters)

    sent = from_own(final)
    mirrored = from_own(jnp.stack([moved(sent[2 * dh + dc], mirror_route(dh, dc)) for dh in range(2) for dc in range(2)]))
    lower_rows = jnp.arange(4)[:, None, None] >= 2
    direct = (k < 4) | (opposite & jnp.where(e < 4, h == 0, lower_rows))
    final = jnp.where(direct, final.transpose(0, 2, 1), mirrored).reshape(rows, quarter)
    return (coeffs[:, None] * final) * column_coeffs[None, :]


def solution(mesh):
    placed = (P("ex", "wa"), P("ex"))
    return jax.shard_map(
        per_device, mesh=mesh, in_specs=placed, out_specs=P("ex", "wa"), check_vma=False
    )
```

```python
import jax
import jax.numpy as jnp
from jax import lax
from jax.experimental import pallas as pl
from jax.experimental.pallas import tpu as pltpu
from jax.sharding import PartitionSpec as P

NB = 8
LANES = 128
FIRST, SECOND, PIECE = 480, 424, 200
TAIL = 8


def moved(value, route):
    pairs = []
    for e in range(NB):
        for w in range(4 * NB):
            to = route(e // 4, e % 4, w // 4, w // 2 % 2, w % 2)
            if to is not None:
                tx, ty, tz, th, tc = to
                pairs.append(((e * 4 * NB) + w, (tx * 4 + ty) * 4 * NB + tz * 4 + th * 2 + tc))
    return lax.ppermute(value, ("ex", "wa"), pairs)


def along_y(value, d):
    return moved(value, lambda x, y, z, h, c: (x, (y + d) % 4, z, h, c))


def along_x(value, d):
    def route(x, y, z, h, c):
        to = (2 * h + x + d) % 4
        return to % 2, y, z, to // 2, c

    return moved(value, route)


def dot_nt(left, right):
    return lax.dot_general(
        left, right, (((1,), (1,)), ((), ())), preferred_element_type=jnp.float32
    )


def power_of_two(n):
    left, size = jnp.abs(n), jnp.ones_like(n)
    for bit in (64.0, 32.0, 16.0, 8.0, 4.0, 2.0, 1.0):
        has = left >= bit
        size = jnp.where(has, size * 2.0**bit, size)
        left = jnp.where(has, left - bit, left)
    return jnp.where(n < 0, 1.0 / size, size)


def products_kernel(core_ref, mine_ref, other_ref, first_ref, second_ref, columns, block, scale, exponent):
    i = pl.program_id(0)
    rows, k = mine_ref.shape[1:]
    quarter, half = rows // 4, rows // 2

    @pl.when(i == 0)
    def _():
        most = jnp.abs(mine_ref[0])
        for j in range(NB):
            most = jnp.maximum(most, jnp.maximum(jnp.abs(mine_ref[j]), jnp.abs(other_ref[j])))
            for h in range(2):
                at = pl.ds(pl.multiple_of(h * half + core_ref[0] * quarter, quarter), quarter)
                a, b = mine_ref[j, at, :], other_ref[j, at, :]
                for copy in (j, j + NB) if j < 4 else (j,):
                    to = pl.ds(copy * quarter, quarter)
                    columns[h, to, :k] = a
                    columns[h, to, k:] = b
        most = jnp.full((TAIL, LANES), jnp.max(most.astype(jnp.float32)))
        bound = jnp.maximum(most * most * (2.0 * k), 1e-30)
        n = jnp.ceil(jnp.log2(bound)) - 11.0
        exponent[...] = n
        scale[...] = power_of_two(-n)

    block[:, :k] = mine_ref[i]
    block[:, k:] = other_ref[i]
    start = pl.multiple_of(i * quarter, quarter)
    factor = scale[0:1, :]
    for h in range(2):
        tile = dot_nt(block[...], columns[h, pl.ds(start, 4 * quarter), :])
        first_ref[0, h, :rows, :] = tile[:, :128] * factor
        first_ref[0, h, rows:FIRST, :64] = tile[:half, 256:] * factor[:, :64]
        first_ref[0, h, rows:FIRST, 64:] = tile[half:, 256:] * factor[:, :64]
        first_ref[0, h, FIRST:, :] = exponent[...]
        second_ref[0, h, :rows, :] = tile[:, 128:256] * factor
        kept = jnp.where(i < 4, h, 1 - h)
        tile = dot_nt(
            columns[h, pl.ds(start + 4 * quarter, quarter), :], block[pl.ds(pl.multiple_of(kept * half, half), half), :]
        )
        second_ref[0, h, rows : rows + 80, :] = tile[:, :128] * factor
        for q in range(3):
            second_ref[0, h, rows + 80 : rows + 104, 32 * q : 32 * q + 32] = (
                tile[24 * q : 24 * q + 24, 128:] * factor[:, :32]
            )
        second_ref[0, h, rows + 80 : rows + 88, 96:] = tile[72:, 128:] * factor[:, :32]
        second_ref[0, h, rows + 88 : rows + 104, 96:] = jnp.zeros((16, 32), jnp.float32)
        second_ref[0, h, SECOND:, :] = exponent[...]


def products(core, mine, other):
    _, rows, k = mine.shape
    whole = pl.BlockSpec(mine.shape, lambda i: (0, 0, 0))
    shapes = [(NB, 2, FIRST + TAIL, LANES), (NB, 2, SECOND + TAIL, LANES)]
    return pl.pallas_call(
        products_kernel,
        grid=(NB,),
        in_specs=[pl.BlockSpec(memory_space=pltpu.SMEM), whole, whole],
        out_specs=[pl.BlockSpec((1,) + s[1:], lambda i: (i, 0, 0, 0)) for s in shapes],
        out_shape=[jax.ShapeDtypeStruct(s, jnp.float32) for s in shapes],
        scratch_shapes=[
            pltpu.VMEM((2, 12 * rows // 4, 2 * k), jnp.bfloat16),
            pltpu.VMEM((rows, 2 * k), jnp.bfloat16),
            pltpu.VMEM((TAIL, LANES), jnp.float32),
            pltpu.VMEM((TAIL, LANES), jnp.float32),
        ],
        compiler_params=pltpu.CompilerParams(vmem_limit_bytes=40 * 1024 * 1024),
        cost_estimate=pl.CostEstimate(
            flops=2 * NB * 9 * rows // 4 * rows * 2 * k, bytes_accessed=NB * rows * (k * 4 + 9 * rows), transcendentals=0
        ),
    )(core, mine, other)


def pieces_kernel(first_ref, second_ref, out_ref, tile):
    rows, half = 320, 160
    tile[0:128, :] = first_ref[:rows, :].T
    tile[128:256, :] = second_ref[:rows, :].T
    packed = first_ref[rows:FIRST, :].T
    tile[256:320, :half] = packed[:64]
    tile[256:320, half:] = packed[64:]
    for p in range(4):
        piece = tile[p * 80 : (p + 1) * 80, :]
        out_ref[p, 0:80, :] = piece[:, :128]
        out_ref[p, 80:160, :] = piece[:, 128:256]
        out_ref[p, 160:200, :64] = piece[:40, 256:]
        out_ref[p, 160:200, 64:] = piece[40:, 256:]
    out_ref[4, :104, :] = second_ref[rows:SECOND, :]
    out_ref[4, 104:, :] = jnp.zeros((96, LANES), jnp.float32)


def pieces_of(first, second):
    return pl.pallas_call(
        pieces_kernel,
        out_shape=jax.ShapeDtypeStruct((5, PIECE, LANES), jnp.float32),
        scratch_shapes=[pltpu.VMEM((320, 320), jnp.float32)],
        cost_estimate=pl.CostEstimate(flops=0, bytes_accessed=1_000_000, transcendentals=0),
    )(first, second)


def exponent_of(array):
    return array.reshape(-1, LANES)[-1:, :1].astype(jnp.float32)


def total_of(arrays, n):
    return sum(a.astype(jnp.float32) * power_of_two(exponent_of(a) - n) for a in arrays)


def exponent_over(arrays):
    most = exponent_of(arrays[0])
    for array in arrays[1:]:
        most = jnp.maximum(most, exponent_of(array))
    return most + 2.0


def with_scale(values, n, dtype):
    is_tail = lax.broadcasted_iota(jnp.int32, values.shape, values.ndim - 2) >= values.shape[-2] - TAIL
    return jnp.where(is_tail, n, values).astype(dtype)


def summed(arrays, dtype=jnp.float32):
    n = exponent_over(arrays)
    return with_scale(total_of(arrays, n), n, dtype)


def per_device(gradients, coeffs):
    rows, width = gradients.shape
    quarter, half = rows // 4, rows // 2
    e = lax.axis_index("ex")
    w = lax.axis_index("wa")
    x, y = e // 4, e % 4
    z, h, c = w // 4, w // 2 % 2, w % 2
    ring = 2 * h + x

    mine = lax.all_to_all(gradients.reshape(rows, NB, width // NB), "ex", 1, 0)
    other = moved(mine, lambda x, y, z, h, c: (x, y, z, h, 1 - c))
    column_coeffs = moved(coeffs, lambda x, y, z, h, c: (z // 4, z % 4, 4 * x + y, h, c))
    column_coeffs = lax.dynamic_slice_in_dim(column_coeffs, (w % 4) * quarter, quarter)

    first, second = products(jnp.reshape(c, (1,)).astype(jnp.int32), mine, other)

    first = first.reshape(2, 4, 2, FIRST + TAIL, LANES)
    second = second.reshape(2, 4, 2, SECOND + TAIL, LANES)

    def for_y(d):
        return lax.dynamic_slice_in_dim(first, (y + d) % 4, 1, 1)[:, 0]

    def for_x(array, d):
        to = (ring + d) % 4
        array = lax.dynamic_index_in_dim(array, to % 2, 0, keepdims=False)
        return lax.dynamic_index_in_dim(array, to // 2, array.ndim - 3, keepdims=False)

    second_there = [along_x(for_x(second, d).astype(jnp.float16), d) for d in (2, 1, 3)]
    first_there = [along_y(for_y(d).astype(jnp.float16), d) for d in (2, 1, 3)]
    second = summed([for_x(second, 0)] + second_there)
    first = summed([for_y(0)] + first_there)

    second_there = [
        along_y(lax.dynamic_index_in_dim(second, (y + d) % 4, 0, keepdims=False).astype(jnp.float16), d) for d in (2, 1, 3)
    ]
    first_there = [along_x(for_x(first, d).astype(jnp.float16), d) for d in (2, 1, 3)]
    first_all = [for_x(first, 0)] + first_there
    second_all = [lax.dynamic_index_in_dim(second, y, 0, keepdims=False)] + second_there
    n = exponent_over(first_all + second_all)
    pieces = pieces_of(total_of(first_all, n), total_of(second_all, n))

    pieces = jnp.pad(pieces, ((0, 3), (0, TAIL), (0, 0)))
    pieces = with_scale(pieces, n, jnp.float16)
    pieces = lax.dynamic_slice_in_dim(jnp.concatenate([pieces, pieces], 0), (NB - e) % NB, NB, 0)
    groups = [[zz * 4 + at for zz in range(NB)] for at in range(4)]
    parts = lax.all_to_all(pieces, "wa", 0, 0, axis_index_groups=groups)
    factors = power_of_two(parts[:, -1:, :1].astype(jnp.float32))
    final = jnp.sum(parts[:, :-TAIL].astype(jnp.float32) * factors, 0)

    normal = jnp.concatenate(
        [final[:80], final[80:160], jnp.concatenate([final[160:, :64], final[160:, 64:]], 0)], 1
    )
    rest = [final[80:104, 0:32], final[80:104, 32:64], final[80:104, 64:96], final[80:88, 96:]]
    kept = jnp.concatenate([final[:80], jnp.concatenate(rest, 0)], 1)
    kept = jnp.concatenate([kept, kept], 1)
    k = (z - e) % NB
    kept_half = jnp.where(e < 4, h, 1 - h)
    final = jnp.where(k == 4, kept, normal).reshape(quarter, 4, quarter).transpose(1, 0, 2)

    def mirror_route(dh, dc):
        def route(x, y, z, h, c):
            e, k = 4 * x + y, (z - 4 * x - y) % NB
            sends = k in (1, 2, 3) or (k == 4 and dh == x)
            return (z // 4, z % 4, e, h ^ dh, c ^ dc) if sends else None

        return route

    def from_own(quarters):
        quarters = jnp.where(c == 1, jnp.stack([quarters[1], quarters[0], quarters[3], quarters[2]]), quarters)
        return jnp.where(h == 1, jnp.stack([quarters[2], quarters[3], quarters[0], quarters[1]]), quarters)

    sent = from_own(final)
    mirrored = from_own(jnp.stack([moved(sent[2 * dh + dc], mirror_route(dh, dc)) for dh in range(2) for dc in range(2)]))
    halves = jnp.arange(4)[:, None, None] // 2
    direct = (k < 4) | ((k == 4) & (halves == kept_half))
    final = jnp.where(direct, final.transpose(0, 2, 1), mirrored).reshape(rows, quarter)
    return (coeffs[:, None] * final) * column_coeffs[None, :]


def solution(mesh):
    placed = (P("ex", "wa"), P("ex"))
    return jax.shard_map(
        per_device, mesh=mesh, in_specs=placed, out_specs=P("ex", "wa"), check_vma=False
    )
```

```python
import jax
import jax.numpy as jnp
from jax import lax
from jax.experimental import pallas as pl
from jax.experimental.pallas import tpu as pltpu
from jax.sharding import PartitionSpec as P

NB = 8
LANES = 128
FIRST, SECOND, PIECE = 480, 424, 200
TAIL = 8


def moved(value, route):
    pairs = []
    for e in range(NB):
        for w in range(4 * NB):
            to = route(e // 4, e % 4, w // 4, w // 2 % 2, w % 2)
            if to is not None:
                tx, ty, tz, th, tc = to
                pairs.append(((e * 4 * NB) + w, (tx * 4 + ty) * 4 * NB + tz * 4 + th * 2 + tc))
    return lax.ppermute(value, ("ex", "wa"), pairs)


def along_y(value):
    return lax.all_to_all(value, "ex", 0, 0, axis_index_groups=[[0, 1, 2, 3], [4, 5, 6, 7]])


def along_x(value, d):
    def route(x, y, z, h, c):
        to = (2 * h + x + d) % 4
        return to % 2, y, z, to // 2, c

    return moved(value, route)


def dot_nt(left, right):
    return lax.dot_general(
        left, right, (((1,), (1,)), ((), ())), preferred_element_type=jnp.float32
    )


def power_of_two(n):
    left, size = jnp.abs(n), jnp.ones_like(n)
    for bit in (64.0, 32.0, 16.0, 8.0, 4.0, 2.0, 1.0):
        has = left >= bit
        size = jnp.where(has, size * 2.0**bit, size)
        left = jnp.where(has, left - bit, left)
    return jnp.where(n < 0, 1.0 / size, size)


def products_kernel(core_ref, mine_ref, other_ref, first_ref, second_ref, columns, block, scale, exponent):
    i = pl.program_id(0)
    rows, k = mine_ref.shape[1:]
    quarter, half = rows // 4, rows // 2

    @pl.when(i == 0)
    def _():
        most = jnp.abs(mine_ref[0])
        for j in range(NB):
            most = jnp.maximum(most, jnp.maximum(jnp.abs(mine_ref[j]), jnp.abs(other_ref[j])))
            for h in range(2):
                at = pl.ds(pl.multiple_of(h * half + core_ref[0] * quarter, quarter), quarter)
                a, b = mine_ref[j, at, :], other_ref[j, at, :]
                for copy in (j, j + NB) if j < 4 else (j,):
                    to = pl.ds(copy * quarter, quarter)
                    columns[h, to, :k] = a
                    columns[h, to, k:] = b
        most = jnp.full((TAIL, LANES), jnp.max(most.astype(jnp.float32)))
        bound = jnp.maximum(most * most * (2.0 * k), 1e-30)
        n = jnp.ceil(jnp.log2(bound)) - 11.0
        exponent[...] = n
        scale[...] = power_of_two(-n)

    block[:, :k] = mine_ref[i]
    block[:, k:] = other_ref[i]
    start = pl.multiple_of(i * quarter, quarter)
    factor = scale[0:1, :]
    for h in range(2):
        tile = dot_nt(block[...], columns[h, pl.ds(start, 4 * quarter), :])
        first_ref[0, 0, h, :rows, :] = tile[:, :128] * factor
        first_ref[0, 0, h, rows:FIRST, :64] = tile[:half, 256:] * factor[:, :64]
        first_ref[0, 0, h, rows:FIRST, 64:] = tile[half:, 256:] * factor[:, :64]
        first_ref[0, 0, h, FIRST:, :] = exponent[...]
        second_ref[0, 0, h, :rows, :] = tile[:, 128:256] * factor
        kept = jnp.where(i < 4, h, 1 - h)
        tile = dot_nt(
            columns[h, pl.ds(start + 4 * quarter, quarter), :], block[pl.ds(pl.multiple_of(kept * half, half), half), :]
        )
        second_ref[0, 0, h, rows : rows + 80, :] = tile[:, :128] * factor
        for q in range(3):
            second_ref[0, 0, h, rows + 80 : rows + 104, 32 * q : 32 * q + 32] = (
                tile[24 * q : 24 * q + 24, 128:] * factor[:, :32]
            )
        second_ref[0, 0, h, rows + 80 : rows + 88, 96:] = tile[72:, 128:] * factor[:, :32]
        second_ref[0, 0, h, rows + 88 : rows + 104, 96:] = jnp.zeros((16, 32), jnp.float32)
        second_ref[0, 0, h, SECOND:, :] = exponent[...]


def products(core, mine, other):
    _, rows, k = mine.shape
    whole = pl.BlockSpec(mine.shape, lambda i: (0, 0, 0))
    shapes = [(4, 2, 2, FIRST + TAIL, LANES), (4, 2, 2, SECOND + TAIL, LANES)]
    return pl.pallas_call(
        products_kernel,
        grid=(NB,),
        in_specs=[pl.BlockSpec(memory_space=pltpu.SMEM), whole, whole],
        out_specs=[pl.BlockSpec((1, 1) + s[2:], lambda i: (i % 4, i // 4, 0, 0, 0)) for s in shapes],
        out_shape=[jax.ShapeDtypeStruct(s, jnp.float32) for s in shapes],
        scratch_shapes=[
            pltpu.VMEM((2, 12 * rows // 4, 2 * k), jnp.bfloat16),
            pltpu.VMEM((rows, 2 * k), jnp.bfloat16),
            pltpu.VMEM((TAIL, LANES), jnp.float32),
            pltpu.VMEM((TAIL, LANES), jnp.float32),
        ],
        compiler_params=pltpu.CompilerParams(vmem_limit_bytes=40 * 1024 * 1024),
        cost_estimate=pl.CostEstimate(
            flops=2 * NB * 9 * rows // 4 * rows * 2 * k, bytes_accessed=NB * rows * (k * 4 + 9 * rows), transcendentals=0
        ),
    )(core, mine, other)


def pieces_kernel(e_ref, first_ref, second_ref, n_ref, out_ref, tile):
    rows, half = 320, 160
    tile[0:128, :] = first_ref[:rows, :].T
    tile[128:256, :] = second_ref[:rows, :].T
    packed = first_ref[rows:FIRST, :].T
    tile[256:320, :half] = packed[:64]
    tile[256:320, half:] = packed[64:]
    for k in range(NB):
        at = (e_ref[0] + k) & (NB - 1)
        if k < 4:
            piece = tile[k * 80 : (k + 1) * 80, :]
            out_ref[at, 0:80, :] = piece[:, :128]
            out_ref[at, 80:160, :] = piece[:, 128:256]
            out_ref[at, 160:200, :64] = piece[:40, 256:]
            out_ref[at, 160:200, 64:] = piece[40:, 256:]
        elif k == 4:
            out_ref[at, :104, :] = second_ref[rows:SECOND, :]
            out_ref[at, 104:PIECE, :] = jnp.zeros((PIECE - 104, LANES), jnp.float32)
        else:
            out_ref[at, :PIECE, :] = jnp.zeros((PIECE, LANES), jnp.float32)
        out_ref[at, PIECE:, :] = n_ref[...]


def pieces_of(e, first, second, n):
    vmem = pl.BlockSpec(memory_space=pltpu.VMEM)
    return pl.pallas_call(
        pieces_kernel,
        in_specs=[pl.BlockSpec(memory_space=pltpu.SMEM), vmem, vmem, vmem],
        out_specs=vmem,
        out_shape=jax.ShapeDtypeStruct((NB, PIECE + TAIL, LANES), jnp.float32),
        scratch_shapes=[pltpu.VMEM((320, 320), jnp.float32)],
        cost_estimate=pl.CostEstimate(flops=0, bytes_accessed=1_300_000, transcendentals=0),
    )(e, first, second, n)


def tail_of(array):
    return array.reshape(-1, array.shape[-2], LANES)[0, -TAIL:, :].astype(jnp.float32)


def scales_of(arrays):
    tails = jnp.stack([tail_of(a) for a in arrays])
    n = jnp.max(tails, 0) + 2.0
    n, factors = lax.optimization_barrier((n, power_of_two(tails - n)))
    return n, [factors[s, :1] for s in range(len(arrays))]


def total_of(arrays, factors):
    return sum(a.astype(jnp.float32) * f for a, f in zip(arrays, factors))


def summed(arrays):
    n, factors = scales_of(arrays)
    total = total_of(arrays, factors)
    is_tail = lax.broadcasted_iota(jnp.int32, total.shape, total.ndim - 2) >= total.shape[-2] - TAIL
    return jnp.where(is_tail, n[:1], total)


def per_device(gradients, coeffs):
    rows, width = gradients.shape
    quarter, half = rows // 4, rows // 2
    e = lax.axis_index("ex")
    w = lax.axis_index("wa")
    x, y = e >> 2, e & 3
    z, h, c = w >> 2, (w >> 1) & 1, w & 1
    ring = 2 * h + x

    mine = lax.all_to_all(gradients.reshape(rows, NB, width // NB), "ex", 1, 0)
    other = moved(mine, lambda x, y, z, h, c: (x, y, z, h, 1 - c))
    column_coeffs = moved(coeffs, lambda x, y, z, h, c: (z // 4, z % 4, 4 * x + y, h, c))
    column_coeffs = lax.dynamic_slice_in_dim(column_coeffs, (w & 3) * quarter, quarter)

    first, second = products(jnp.reshape(c, (1,)).astype(jnp.int32), mine, other)

    def for_x(array, d):
        to = (ring + d) & 3
        array = lax.dynamic_index_in_dim(array, to & 1, array.ndim - 4, keepdims=False)
        return lax.dynamic_index_in_dim(array, to >> 1, array.ndim - 3, keepdims=False)

    def all_along_x(array):
        return [for_x(array, 0)] + [along_x(for_x(array, d).astype(jnp.float16), d) for d in (2, 1, 3)]

    def all_along_y(array):
        array = along_y(array.astype(jnp.float16))
        return [array[s] for s in range(4)]

    first_all, second_all = all_along_y(first), all_along_x(second)
    first, second = summed(first_all), summed(second_all)
    first_all, second_all = all_along_x(first), all_along_y(second)
    n, factors = scales_of(first_all + second_all)
    pieces = pieces_of(
        jnp.reshape(e, (1,)).astype(jnp.int32), total_of(first_all, factors[:4]), total_of(second_all, factors[4:]), n
    )

    groups = [[zz * 4 + at for zz in range(NB)] for at in range(4)]
    parts = lax.all_to_all(pieces.astype(jnp.float16), "wa", 0, 0, axis_index_groups=groups)
    factors = power_of_two(parts[:, -1:, :1].astype(jnp.float32))
    final = jnp.sum(parts[:, :-TAIL].astype(jnp.float32) * factors, 0)

    normal = jnp.concatenate(
        [final[:80], final[80:160], jnp.concatenate([final[160:, :64], final[160:, 64:]], 0)], 1
    )
    rest = [final[80:104, 0:32], final[80:104, 32:64], final[80:104, 64:96], final[80:88, 96:]]
    kept = jnp.concatenate([final[:80], jnp.concatenate(rest, 0)], 1)
    kept = jnp.concatenate([kept, kept], 1)
    k = (z - e) & (NB - 1)
    kept_half = jnp.where(e < 4, h, 1 - h)
    final = jnp.where(k == 4, kept, normal).reshape(quarter, 4, quarter).transpose(1, 0, 2)

    def mirror_route(dh, dc):
        def route(x, y, z, h, c):
            e, k = 4 * x + y, (z - 4 * x - y) % NB
            sends = k in (1, 2, 3) or (k == 4 and dh == x)
            return (z // 4, z % 4, e, h ^ dh, c ^ dc) if sends else None

        return route

    def from_own(quarters):
        quarters = jnp.where(c == 1, jnp.stack([quarters[1], quarters[0], quarters[3], quarters[2]]), quarters)
        return jnp.where(h == 1, jnp.stack([quarters[2], quarters[3], quarters[0], quarters[1]]), quarters)

    sent = from_own(final)
    mirrored = from_own(jnp.stack([moved(sent[2 * dh + dc], mirror_route(dh, dc)) for dh in range(2) for dc in range(2)]))
    halves = jnp.arange(4)[:, None, None] // 2
    direct = (k < 4) | ((k == 4) & (halves == kept_half))
    final = jnp.where(direct, final.transpose(0, 2, 1), mirrored).reshape(rows, quarter)
    return (coeffs[:, None] * final) * column_coeffs[None, :]


def solution(mesh):
    placed = (P("ex", "wa"), P("ex"))
    return jax.shard_map(
        per_device, mesh=mesh, in_specs=placed, out_specs=P("ex", "wa"), check_vma=False
    )
```

```python
import jax
import jax.numpy as jnp
from jax import lax
from jax.experimental import pallas as pl
from jax.experimental.pallas import tpu as pltpu
from jax.sharding import PartitionSpec as P

NB = 8
LANES = 128
FIRST, SECOND, PIECE = 480, 424, 200
TAIL = 8


def moved(value, route):
    pairs = []
    for e in range(NB):
        for w in range(4 * NB):
            to = route(e // 4, e % 4, w // 4, w // 2 % 2, w % 2)
            if to is not None:
                tx, ty, tz, th, tc = to
                pairs.append(((e * 4 * NB) + w, (tx * 4 + ty) * 4 * NB + tz * 4 + th * 2 + tc))
    return lax.ppermute(value, ("ex", "wa"), pairs)


def along_y(value):
    return lax.all_to_all(value, "ex", 0, 0, axis_index_groups=[[0, 1, 2, 3], [4, 5, 6, 7]])


def along_x(value, d):
    def route(x, y, z, h, c):
        to = (2 * h + x + d) % 4
        return to % 2, y, z, to // 2, c

    return moved(value, route)


def dot_nt(left, right):
    return lax.dot_general(
        left, right, (((1,), (1,)), ((), ())), preferred_element_type=jnp.float32
    )


def power_of_two(n):
    left, size = jnp.abs(n), jnp.ones_like(n)
    for bit in (64.0, 32.0, 16.0, 8.0, 4.0, 2.0, 1.0):
        has = left >= bit
        size = jnp.where(has, size * 2.0**bit, size)
        left = jnp.where(has, left - bit, left)
    return jnp.where(n < 0, 1.0 / size, size)


def products_kernel(core_ref, scale_ref, mine_ref, other_ref, first_ref, second_ref, held, columns, arrived):
    i = pl.program_id(0)
    rows, k = mine_ref.shape[1:]
    quarter, half = rows // 4, rows // 2

    def fetches(j):
        return [
            pltpu.make_async_copy(ref.at[j], held.at[j, :, pl.ds(part * k, k)], arrived.at[part, j])
            for part, ref in enumerate((mine_ref, other_ref))
        ]

    def take(j):
        for fetch in fetches(j):
            fetch.wait()
        for h in range(2):
            at = pl.ds(pl.multiple_of(h * half + core_ref[0] * quarter, quarter), quarter)
            own = held[j, at, :]
            columns[h, pl.ds(j * quarter, quarter), :] = own
            if j < 4:
                columns[h, pl.ds((j + NB) * quarter, quarter), :] = own

    @pl.when(i == 0)
    def _():
        for j in range(NB):
            for fetch in fetches(j):
                fetch.start()
        for j in range(5):
            take(j)

    for later in range(1, 4):

        @pl.when(i == later)
        def _():
            take(later + 4)

    start = pl.multiple_of(i * quarter, quarter)
    factor = scale_ref[1, 0:1, :]
    for h in range(2):
        tile = dot_nt(held[i], columns[h, pl.ds(start, 5 * quarter), :])
        first_ref[0, 0, h, :rows, :] = tile[:, :128] * factor
        first_ref[0, 0, h, rows:FIRST, :64] = tile[:half, 256:320] * factor[:, :64]
        first_ref[0, 0, h, rows:FIRST, 64:] = tile[half:, 256:320] * factor[:, :64]
        first_ref[0, 0, h, FIRST:, :] = scale_ref[0]
        second_ref[0, 0, h, :rows, :] = tile[:, 128:256] * factor
        kept = jnp.where((i < 4) == (h == 0), tile[:half, 256:], tile[half:, 256:]).T[64:]
        second_ref[0, 0, h, rows : rows + 80, :] = kept[:, :128] * factor
        for q in range(3):
            second_ref[0, 0, h, rows + 80 : rows + 104, 32 * q : 32 * q + 32] = (
                kept[24 * q : 24 * q + 24, 128:] * factor[:, :32]
            )
        second_ref[0, 0, h, rows + 80 : rows + 88, 96:] = kept[72:, 128:] * factor[:, :32]
        second_ref[0, 0, h, rows + 88 : rows + 104, 96:] = jnp.zeros((16, 32), jnp.float32)
        second_ref[0, 0, h, SECOND:, :] = scale_ref[0]


def products(core, scale, mine, other):
    _, rows, k = mine.shape
    shapes = [(4, 2, 2, FIRST + TAIL, LANES), (4, 2, 2, SECOND + TAIL, LANES)]
    anywhere = pl.BlockSpec(memory_space=pl.ANY)
    return pl.pallas_call(
        products_kernel,
        grid=(NB,),
        in_specs=[
            pl.BlockSpec(memory_space=pltpu.SMEM),
            pl.BlockSpec(scale.shape, lambda i: (0, 0, 0)),
            anywhere,
            anywhere,
        ],
        out_specs=[pl.BlockSpec((1, 1) + s[2:], lambda i: (i % 4, i // 4, 0, 0, 0)) for s in shapes],
        out_shape=[jax.ShapeDtypeStruct(s, jnp.float32) for s in shapes],
        scratch_shapes=[
            pltpu.VMEM((NB, rows, 2 * k), jnp.bfloat16),
            pltpu.VMEM((2, 12 * rows // 4, 2 * k), jnp.bfloat16),
            pltpu.SemaphoreType.DMA((2, NB)),
        ],
        compiler_params=pltpu.CompilerParams(vmem_limit_bytes=20 * 1024 * 1024),
        cost_estimate=pl.CostEstimate(
            flops=2 * NB * 9 * rows // 4 * rows * 2 * k, bytes_accessed=NB * rows * (k * 4 + 9 * rows), transcendentals=0
        ),
    )(core, scale, mine, other)


def pieces_kernel(e_ref, first_ref, second_ref, n_ref, out_ref, tile):
    rows, half = 320, 160
    tile[0:128, :] = first_ref[:rows, :].T
    tile[128:256, :] = second_ref[:rows, :].T
    packed = first_ref[rows:FIRST, :].T
    tile[256:320, :half] = packed[:64]
    tile[256:320, half:] = packed[64:]
    for k in range(NB):
        at = (e_ref[0] + k) & (NB - 1)
        if k < 4:
            piece = tile[k * 80 : (k + 1) * 80, :]
            out_ref[at, 0:80, :] = piece[:, :128]
            out_ref[at, 80:160, :] = piece[:, 128:256]
            out_ref[at, 160:200, :64] = piece[:40, 256:]
            out_ref[at, 160:200, 64:] = piece[40:, 256:]
        elif k == 4:
            out_ref[at, :104, :] = second_ref[rows:SECOND, :]
            out_ref[at, 104:PIECE, :] = jnp.zeros((PIECE - 104, LANES), jnp.float32)
        else:
            out_ref[at, :PIECE, :] = jnp.zeros((PIECE, LANES), jnp.float32)
        out_ref[at, PIECE:, :] = n_ref[...]


def pieces_of(e, first, second, n):
    vmem = pl.BlockSpec(memory_space=pltpu.VMEM)
    return pl.pallas_call(
        pieces_kernel,
        in_specs=[pl.BlockSpec(memory_space=pltpu.SMEM), vmem, vmem, vmem],
        out_specs=vmem,
        out_shape=jax.ShapeDtypeStruct((NB, PIECE + TAIL, LANES), jnp.float32),
        scratch_shapes=[pltpu.VMEM((320, 320), jnp.float32)],
        cost_estimate=pl.CostEstimate(flops=0, bytes_accessed=1_300_000, transcendentals=0),
    )(e, first, second, n)


def tail_of(array):
    return array.reshape(-1, array.shape[-2], LANES)[0, -TAIL:, :].astype(jnp.float32)


def scales_of(arrays):
    tails = jnp.stack([tail_of(a) for a in arrays])
    n = jnp.max(tails, 0) + 2.0
    n, factors = lax.optimization_barrier((n, power_of_two(tails - n)))
    return n, [factors[s, :1] for s in range(len(arrays))]


def total_of(arrays, factors):
    return sum(a.astype(jnp.float32) * f for a, f in zip(arrays, factors))


def summed(arrays):
    n, factors = scales_of(arrays)
    total = total_of(arrays, factors)
    is_tail = lax.broadcasted_iota(jnp.int32, total.shape, total.ndim - 2) >= total.shape[-2] - TAIL
    return jnp.where(is_tail, n[:1], total)


def per_device(gradients, coeffs):
    rows, width = gradients.shape
    quarter, half = rows // 4, rows // 2
    e = lax.axis_index("ex")
    w = lax.axis_index("wa")
    x, y = e >> 2, e & 3
    z, h, c = w >> 2, (w >> 1) & 1, w & 1
    ring = 2 * h + x

    mine = lax.all_to_all(gradients.reshape(rows, NB, width // NB), "ex", 1, 0)
    other = moved(mine, lambda x, y, z, h, c: (x, y, z, h, 1 - c))
    column_coeffs = moved(coeffs, lambda x, y, z, h, c: (z // 4, z % 4, 4 * x + y, h, c))
    column_coeffs = lax.dynamic_slice_in_dim(column_coeffs, (w & 3) * quarter, quarter)

    most = jnp.broadcast_to(jnp.max(jnp.abs(mine)).astype(jnp.float32), (TAIL, LANES))
    most = jnp.maximum(most, moved(most, lambda x, y, z, h, c: (x, y, z, h, 1 - c)))
    bound = jnp.maximum(most * most * (2.0 * width / NB), 1e-30)
    n = jnp.ceil(jnp.log2(bound)) - 11.0
    scale = jnp.stack([n, power_of_two(-n)])

    first, second = products(jnp.reshape(c, (1,)).astype(jnp.int32), scale, mine, other)

    def for_x(array, d):
        to = (ring + d) & 3
        array = lax.dynamic_index_in_dim(array, to & 1, array.ndim - 4, keepdims=False)
        return lax.dynamic_index_in_dim(array, to >> 1, array.ndim - 3, keepdims=False)

    def all_along_x(array):
        return [for_x(array, 0)] + [along_x(for_x(array, d).astype(jnp.float16), d) for d in (2, 1, 3)]

    def all_along_y(array):
        array = along_y(array.astype(jnp.float16))
        return [array[s] for s in range(4)]

    first, second = lax.optimization_barrier((first.astype(jnp.float16), second))
    first_all, second_all = all_along_y(first), all_along_x(second)
    first, second = summed(first_all), summed(second_all)
    first_all, second_all = all_along_x(first), all_along_y(second)
    n, factors = scales_of(first_all + second_all)
    pieces = pieces_of(
        jnp.reshape(e, (1,)).astype(jnp.int32), total_of(first_all, factors[:4]), total_of(second_all, factors[4:]), n
    )

    groups = [[zz * 4 + at for zz in range(NB)] for at in range(4)]
    parts = lax.all_to_all(pieces.astype(jnp.float16), "wa", 0, 0, axis_index_groups=groups)
    factors = power_of_two(parts[:, -1:, :1].astype(jnp.float32))
    final = jnp.sum(parts[:, :-TAIL].astype(jnp.float32) * factors, 0)

    normal = jnp.concatenate(
        [final[:80], final[80:160], jnp.concatenate([final[160:, :64], final[160:, 64:]], 0)], 1
    )
    rest = [final[80:104, 0:32], final[80:104, 32:64], final[80:104, 64:96], final[80:88, 96:]]
    kept = jnp.concatenate([final[:80], jnp.concatenate(rest, 0)], 1)
    kept = jnp.concatenate([kept, kept], 1)
    k = (z - e) & (NB - 1)
    kept_half = jnp.where(e < 4, h, 1 - h)
    final = jnp.where(k == 4, kept, normal).reshape(quarter, 4, quarter).transpose(1, 0, 2)

    def mirror_route(dh, dc):
        def route(x, y, z, h, c):
            e, k = 4 * x + y, (z - 4 * x - y) % NB
            sends = k in (1, 2, 3) or (k == 4 and dh == x)
            return (z // 4, z % 4, e, h ^ dh, c ^ dc) if sends else None

        return route

    def from_own(quarters):
        quarters = jnp.where(c == 1, jnp.stack([quarters[1], quarters[0], quarters[3], quarters[2]]), quarters)
        return jnp.where(h == 1, jnp.stack([quarters[2], quarters[3], quarters[0], quarters[1]]), quarters)

    sent = from_own(final)
    mirrored = from_own(jnp.stack([moved(sent[2 * dh + dc], mirror_route(dh, dc)) for dh in range(2) for dc in range(2)]))
    halves = jnp.arange(4)[:, None, None] // 2
    direct = (k < 4) | ((k == 4) & (halves == kept_half))
    final = jnp.where(direct, final.transpose(0, 2, 1), mirrored).reshape(rows, quarter)
    return (coeffs[:, None] * final) * column_coeffs[None, :]


def solution(mesh):
    placed = (P("ex", "wa"), P("ex"))
    return jax.shard_map(
        per_device, mesh=mesh, in_specs=placed, out_specs=P("ex", "wa"), check_vma=False
    )
```

```python
import jax
import jax.numpy as jnp
from jax import lax
from jax.experimental import pallas as pl
from jax.experimental.pallas import tpu as pltpu
from jax.sharding import PartitionSpec as P

NB = 8
LANES = 128
FIRST, SECOND, PIECE = 424, 480, 200
TAIL = 8


def moved(value, route):
    pairs = []
    for e in range(NB):
        for w in range(4 * NB):
            to = route(e // 4, e % 4, w // 4, w // 2 % 2, w % 2)
            if to is not None:
                tx, ty, tz, th, tc = to
                pairs.append(((e * 4 * NB) + w, (tx * 4 + ty) * 4 * NB + tz * 4 + th * 2 + tc))
    return lax.ppermute(value, ("ex", "wa"), pairs)


def along_y(value, d):
    return moved(value, lambda x, y, z, h, c: (x, (y + d) % 4, z, h, c))


def along_x(value, d):
    def route(x, y, z, h, c):
        to = (2 * h + x + d) % 4
        return to % 2, y, z, to // 2, c

    return moved(value, route)


def dot_nt(left, right):
    return lax.dot_general(
        left, right, (((1,), (1,)), ((), ())), preferred_element_type=jnp.float32
    )


def power_of_two(n):
    left, size = jnp.abs(n), jnp.ones_like(n)
    for bit in (64.0, 32.0, 16.0, 8.0, 4.0, 2.0, 1.0):
        has = left >= bit
        size = jnp.where(has, size * 2.0**bit, size)
        left = jnp.where(has, left - bit, left)
    return jnp.where(n < 0, 1.0 / size, size)


def products_kernel(core_ref, scale_ref, mine_ref, other_ref, first_ref, second_ref, held, columns, arrived):
    i = pl.program_id(0)
    rows, k = mine_ref.shape[1:]
    quarter, half = rows // 4, rows // 2

    def fetches(j):
        return [
            pltpu.make_async_copy(ref.at[j], held.at[j, :, pl.ds(part * k, k)], arrived.at[part, j])
            for part, ref in enumerate((mine_ref, other_ref))
        ]

    def take(j):
        for fetch in fetches(j):
            fetch.wait()
        for h in range(2):
            at = pl.ds(pl.multiple_of(h * half + core_ref[0] * quarter, quarter), quarter)
            own = held[j, at, :]
            columns[h, pl.ds(j * quarter, quarter), :] = own
            if j < 4:
                columns[h, pl.ds((j + NB) * quarter, quarter), :] = own

    @pl.when(i == 0)
    def _():
        for j in range(NB):
            for fetch in fetches(j):
                fetch.start()
        for j in range(5):
            take(j)

    for later in range(1, 4):

        @pl.when(i == later)
        def _():
            take(later + 4)

    start = pl.multiple_of(i * quarter, quarter)
    factor = scale_ref[1, 0:1, :]
    for h in range(2):
        tile = dot_nt(held[i], columns[h, pl.ds(start, 5 * quarter), :])
        first_ref[0, 0, h, :rows, :] = tile[:, :128] * factor
        kept = jnp.where((i < 4) == (h == 0), tile[:half, 256:], tile[half:, 256:]).T[64:]
        first_ref[0, 0, h, rows : rows + 80, :] = kept[:, :128] * factor
        for q in range(3):
            first_ref[0, 0, h, rows + 80 : rows + 104, 32 * q : 32 * q + 32] = (
                kept[24 * q : 24 * q + 24, 128:] * factor[:, :32]
            )
        first_ref[0, 0, h, rows + 80 : rows + 88, 96:] = kept[72:, 128:] * factor[:, :32]
        first_ref[0, 0, h, rows + 88 : rows + 104, 96:] = jnp.zeros((16, 32), jnp.float32)
        first_ref[0, 0, h, FIRST:, :] = scale_ref[0]
        second_ref[0, 0, h, :rows, :] = tile[:, 128:256] * factor
        second_ref[0, 0, h, rows:SECOND, :64] = tile[:half, 256:320] * factor[:, :64]
        second_ref[0, 0, h, rows:SECOND, 64:] = tile[half:, 256:320] * factor[:, :64]
        second_ref[0, 0, h, SECOND:, :] = scale_ref[0]


def products(core, scale, mine, other):
    _, rows, k = mine.shape
    shapes = [(4, 2, 2, FIRST + TAIL, LANES), (4, 2, 2, SECOND + TAIL, LANES)]
    anywhere = pl.BlockSpec(memory_space=pl.ANY)
    return pl.pallas_call(
        products_kernel,
        grid=(NB,),
        in_specs=[
            pl.BlockSpec(memory_space=pltpu.SMEM),
            pl.BlockSpec(scale.shape, lambda i: (0, 0, 0)),
            anywhere,
            anywhere,
        ],
        out_specs=[pl.BlockSpec((1, 1) + s[2:], lambda i: (i % 4, i // 4, 0, 0, 0)) for s in shapes],
        out_shape=[jax.ShapeDtypeStruct(s, jnp.float32) for s in shapes],
        scratch_shapes=[
            pltpu.VMEM((NB, rows, 2 * k), jnp.bfloat16),
            pltpu.VMEM((2, 12 * rows // 4, 2 * k), jnp.bfloat16),
            pltpu.SemaphoreType.DMA((2, NB)),
        ],
        compiler_params=pltpu.CompilerParams(vmem_limit_bytes=20 * 1024 * 1024),
        cost_estimate=pl.CostEstimate(
            flops=2 * NB * 9 * rows // 4 * rows * 2 * k, bytes_accessed=NB * rows * (k * 4 + 9 * rows), transcendentals=0
        ),
    )(core, scale, mine, other)


def pieces_kernel(e_ref, first_ref, second_ref, n_ref, out_ref, tile):
    rows, half = 320, 160
    tile[0:128, :] = first_ref[:rows, :].T
    tile[128:256, :] = second_ref[:rows, :].T
    packed = second_ref[rows:SECOND, :].T
    tile[256:320, :half] = packed[:64]
    tile[256:320, half:] = packed[64:]
    for k in range(NB):
        at = (e_ref[0] + k) & (NB - 1)
        if k < 4:
            piece = tile[k * 80 : (k + 1) * 80, :]
            out_ref[at, 0:80, :] = piece[:, :128]
            out_ref[at, 80:160, :] = piece[:, 128:256]
            out_ref[at, 160:200, :64] = piece[:40, 256:]
            out_ref[at, 160:200, 64:] = piece[40:, 256:]
        elif k == 4:
            out_ref[at, :104, :] = first_ref[rows:FIRST, :]
            out_ref[at, 104:PIECE, :] = jnp.zeros((PIECE - 104, LANES), jnp.float32)
        else:
            out_ref[at, :PIECE, :] = jnp.zeros((PIECE, LANES), jnp.float32)
        out_ref[at, PIECE:, :] = n_ref[...]


def pieces_of(e, first, second, n):
    vmem = pl.BlockSpec(memory_space=pltpu.VMEM)
    return pl.pallas_call(
        pieces_kernel,
        in_specs=[pl.BlockSpec(memory_space=pltpu.SMEM), vmem, vmem, vmem],
        out_specs=vmem,
        out_shape=jax.ShapeDtypeStruct((NB, PIECE + TAIL, LANES), jnp.float32),
        scratch_shapes=[pltpu.VMEM((320, 320), jnp.float32)],
        cost_estimate=pl.CostEstimate(flops=0, bytes_accessed=1_300_000, transcendentals=0),
    )(e, first, second, n)


def tail_of(array):
    return array.reshape(-1, array.shape[-2], LANES)[0, -TAIL:, :].astype(jnp.float32)


def scales_of(arrays):
    tails = [tail_of(a) for a in arrays]
    n = tails[0]
    for tail in tails[1:]:
        n = jnp.maximum(n, tail)
    n = n + 2.0
    n, *factors = lax.optimization_barrier((n, *[power_of_two(t - n) for t in tails]))
    return n, factors


def total_of(arrays, factors):
    return sum(a.astype(jnp.float32) * f[:1] for a, f in zip(arrays, factors))


def with_tail(total, n):
    is_tail = lax.broadcasted_iota(jnp.int32, total.shape, total.ndim - 2) >= total.shape[-2] - TAIL
    return jnp.where(is_tail, n[:1], total)


def per_device(gradients, coeffs):
    rows, width = gradients.shape
    quarter, half = rows // 4, rows // 2
    e = lax.axis_index("ex")
    w = lax.axis_index("wa")
    x, y = e >> 2, e & 3
    z, h, c = w >> 2, (w >> 1) & 1, w & 1
    ring = 2 * h + x

    mine = lax.all_to_all(gradients.reshape(rows, NB, width // NB), "ex", 1, 0)
    other = moved(mine, lambda x, y, z, h, c: (x, y, z, h, 1 - c))
    column_coeffs = moved(coeffs, lambda x, y, z, h, c: (z // 4, z % 4, 4 * x + y, h, c))
    column_coeffs = lax.dynamic_slice_in_dim(column_coeffs, (w & 3) * quarter, quarter)

    most = jnp.broadcast_to(jnp.max(jnp.abs(mine)).astype(jnp.float32), (TAIL, LANES))
    most = jnp.maximum(most, moved(most, lambda x, y, z, h, c: (x, y, z, h, 1 - c)))
    bound = jnp.maximum(most * most * (2.0 * width / NB), 1e-30)
    n = jnp.ceil(jnp.log2(bound)) - 11.0
    scale = jnp.stack([n, power_of_two(-n)])

    first, second = products(jnp.reshape(c, (1,)).astype(jnp.int32), scale, mine, other)

    def for_x(array, d):
        to = (ring + d) & 3
        array = lax.dynamic_index_in_dim(array, to & 1, array.ndim - 4, keepdims=False)
        return lax.dynamic_index_in_dim(array, to >> 1, array.ndim - 3, keepdims=False)

    def for_y(array, d):
        return lax.dynamic_index_in_dim(array, (y + d) & 3, 0, keepdims=False)

    def all_along_x(array):
        return [for_x(array, 0)] + [along_x(for_x(array, d).astype(jnp.float16), d) for d in (2, 1, 3)]

    first, second = lax.optimization_barrier((first.astype(jnp.float16), second))
    first = lax.all_to_all(first, "ex", 0, 0, axis_index_groups=[[0, 1, 2, 3], [4, 5, 6, 7]])
    second_all = all_along_x(second)
    n, factors = scales_of(second_all)
    second = with_tail(total_of(second_all, factors), n)
    second_all = [for_y(second, 0)] + [along_y(for_y(second, d).astype(jnp.float16), d) for d in (2, 1, 3)]
    n, factors = scales_of([first[s] for s in range(4)])
    factors = jnp.stack([f[:1] for f in factors]).reshape(4, 1, 1, 1, LANES)
    first = with_tail(jnp.sum(first.astype(jnp.float32) * factors, 0), n)
    first_all = all_along_x(first)
    n, factors = scales_of(first_all + second_all)
    pieces = pieces_of(
        jnp.reshape(e, (1,)).astype(jnp.int32), total_of(first_all, factors[:4]), total_of(second_all, factors[4:]), n
    )

    def along_z(value, d):
        def route(x, y, z, h, c):
            return (x, y, (z + d) % NB, h, c) if (z + d - 4 * x - y) % NB < 5 else None

        return moved(value, route)

    def for_z(d):
        return lax.dynamic_index_in_dim(pieces, (z + d) & (NB - 1), 0, keepdims=False)

    parts = [for_z(0)] + [along_z(for_z(d).astype(jnp.float16), d) for d in (4, 3, 5, 2, 6, 1, 7)]
    factors = lax.optimization_barrier(tuple(power_of_two(tail_of(p)) for p in parts))
    final = total_of(parts, factors)[:PIECE]

    normal = jnp.concatenate(
        [final[:80], final[80:160], jnp.concatenate([final[160:, :64], final[160:, 64:]], 0)], 1
    )
    rest = [final[80:104, 0:32], final[80:104, 32:64], final[80:104, 64:96], final[80:88, 96:]]
    kept = jnp.concatenate([final[:80], jnp.concatenate(rest, 0)], 1)
    kept = jnp.concatenate([kept, kept], 1)
    k = (z - e) & (NB - 1)
    kept_half = jnp.where(e < 4, h, 1 - h)
    final = jnp.where(k == 4, kept, normal).reshape(quarter, 4, quarter).transpose(1, 0, 2)

    def mirror_route(dh, dc):
        def route(x, y, z, h, c):
            e, k = 4 * x + y, (z - 4 * x - y) % NB
            sends = k in (1, 2, 3) or (k == 4 and dh == x)
            return (z // 4, z % 4, e, h ^ dh, c ^ dc) if sends else None

        return route

    def from_own(quarters):
        quarters = jnp.where(c == 1, jnp.stack([quarters[1], quarters[0], quarters[3], quarters[2]]), quarters)
        return jnp.where(h == 1, jnp.stack([quarters[2], quarters[3], quarters[0], quarters[1]]), quarters)

    sent = from_own(final)
    mirrored = from_own(jnp.stack([moved(sent[2 * dh + dc], mirror_route(dh, dc)) for dh in range(2) for dc in range(2)]))
    halves = jnp.arange(4)[:, None, None] // 2
    direct = (k < 4) | ((k == 4) & (halves == kept_half))
    final = jnp.where(direct, final.transpose(0, 2, 1), mirrored).reshape(rows, quarter)
    return (coeffs[:, None] * final) * column_coeffs[None, :]


def solution(mesh):
    placed = (P("ex", "wa"), P("ex"))
    return jax.shard_map(
        per_device, mesh=mesh, in_specs=placed, out_specs=P("ex", "wa"), check_vma=False
    )
```

```python
import jax
import jax.numpy as jnp
from jax import lax
from jax.experimental import pallas as pl
from jax.experimental.pallas import tpu as pltpu
from jax.sharding import PartitionSpec as P

NB = 8
LANES = 128
FIRST, SECOND, PIECE = 424, 480, 200
TAIL = 8


def moved(value, route):
    pairs = []
    for e in range(NB):
        for w in range(4 * NB):
            to = route(e // 4, e % 4, w // 4, w // 2 % 2, w % 2)
            if to is not None:
                tx, ty, tz, th, tc = to
                pairs.append(((e * 4 * NB) + w, (tx * 4 + ty) * 4 * NB + tz * 4 + th * 2 + tc))
    return lax.ppermute(value, ("ex", "wa"), pairs)


def along_y(value, d):
    return moved(value, lambda x, y, z, h, c: (x, (y + d) % 4, z, h, c))


def along_x(value, d):
    def route(x, y, z, h, c):
        to = (2 * h + x + d) % 4
        return to % 2, y, z, to // 2, c

    return moved(value, route)


def dot_nt(left, right):
    return lax.dot_general(
        left, right, (((1,), (1,)), ((), ())), preferred_element_type=jnp.float32
    )


def power_of_two(n):
    left, size = jnp.abs(n), jnp.ones_like(n)
    for bit in (64.0, 32.0, 16.0, 8.0, 4.0, 2.0, 1.0):
        has = left >= bit
        size = jnp.where(has, size * 2.0**bit, size)
        left = jnp.where(has, left - bit, left)
    return jnp.where(n < 0, 1.0 / size, size)


def products_kernel(core_ref, scale_ref, mine_ref, other_ref, first_ref, second_ref, held, columns, arrived):
    i = pl.program_id(0)
    rows, k = mine_ref.shape[1:]
    quarter, half = rows // 4, rows // 2

    def fetches(j):
        return [
            pltpu.make_async_copy(ref.at[j], held.at[j, :, pl.ds(part * k, k)], arrived.at[part, j])
            for part, ref in enumerate((mine_ref, other_ref))
        ]

    def take(j):
        for fetch in fetches(j):
            fetch.wait()
        for h in range(2):
            at = pl.ds(pl.multiple_of(h * half + core_ref[0] * quarter, quarter), quarter)
            own = held[j, at, :]
            columns[h, pl.ds(j * quarter, quarter), :] = own
            if j < 4:
                columns[h, pl.ds((j + NB) * quarter, quarter), :] = own

    @pl.when(i == 0)
    def _():
        for j in range(NB):
            for fetch in fetches(j):
                fetch.start()
        for j in range(5):
            take(j)

    for later in range(1, 4):

        @pl.when(i == later)
        def _():
            take(later + 4)

    start = pl.multiple_of(i * quarter, quarter)
    factor = scale_ref[1, 0:1, :]
    for h in range(2):
        tile = dot_nt(held[i], columns[h, pl.ds(start, 5 * quarter), :])
        first_ref[0, 0, h, :rows, :] = tile[:, :128] * factor
        kept = jnp.where((i < 4) == (h == 0), tile[:half, 256:], tile[half:, 256:]).T[64:]
        first_ref[0, 0, h, rows : rows + 80, :] = kept[:, :128] * factor
        for q in range(3):
            first_ref[0, 0, h, rows + 80 : rows + 104, 32 * q : 32 * q + 32] = (
                kept[24 * q : 24 * q + 24, 128:] * factor[:, :32]
            )
        first_ref[0, 0, h, rows + 80 : rows + 88, 96:] = kept[72:, 128:] * factor[:, :32]
        first_ref[0, 0, h, rows + 88 : rows + 104, 96:] = jnp.zeros((16, 32), jnp.float32)
        first_ref[0, 0, h, FIRST:, :] = scale_ref[0]
        second_ref[0, 0, h, :rows, :] = tile[:, 128:256] * factor
        second_ref[0, 0, h, rows:SECOND, :64] = tile[:half, 256:320] * factor[:, :64]
        second_ref[0, 0, h, rows:SECOND, 64:] = tile[half:, 256:320] * factor[:, :64]
        second_ref[0, 0, h, SECOND:, :] = scale_ref[0]


def products(core, scale, mine, other):
    _, rows, k = mine.shape
    shapes = [(4, 2, 2, FIRST + TAIL, LANES), (4, 2, 2, SECOND + TAIL, LANES)]
    anywhere = pl.BlockSpec(memory_space=pl.ANY)
    return pl.pallas_call(
        products_kernel,
        grid=(NB,),
        in_specs=[
            pl.BlockSpec(memory_space=pltpu.SMEM),
            pl.BlockSpec(scale.shape, lambda i: (0, 0, 0)),
            anywhere,
            anywhere,
        ],
        out_specs=[pl.BlockSpec((1, 1) + s[2:], lambda i: (i % 4, i // 4, 0, 0, 0)) for s in shapes],
        out_shape=[jax.ShapeDtypeStruct(s, jnp.float32) for s in shapes],
        scratch_shapes=[
            pltpu.VMEM((NB, rows, 2 * k), jnp.bfloat16),
            pltpu.VMEM((2, 12 * rows // 4, 2 * k), jnp.bfloat16),
            pltpu.SemaphoreType.DMA((2, NB)),
        ],
        compiler_params=pltpu.CompilerParams(vmem_limit_bytes=20 * 1024 * 1024),
        cost_estimate=pl.CostEstimate(
            flops=2 * NB * 9 * rows // 4 * rows * 2 * k, bytes_accessed=NB * rows * (k * 4 + 9 * rows), transcendentals=0
        ),
    )(core, scale, mine, other)


def pieces_kernel(e_ref, first_ref, second_ref, n_ref, out_ref, tile):
    rows, half = 320, 160
    tile[0:128, :] = first_ref[:rows, :].T
    tile[128:256, :] = second_ref[:rows, :].T
    packed = second_ref[rows:SECOND, :].T
    tile[256:320, :half] = packed[:64]
    tile[256:320, half:] = packed[64:]
    for k in range(NB):
        at = (e_ref[0] + k) & (NB - 1)
        if k < 4:
            piece = tile[k * 80 : (k + 1) * 80, :]
            out_ref[at, 0:80, :] = piece[:, :128]
            out_ref[at, 80:160, :] = piece[:, 128:256]
            out_ref[at, 160:200, :64] = piece[:40, 256:]
            out_ref[at, 160:200, 64:] = piece[40:, 256:]
        elif k == 4:
            out_ref[at, :104, :] = first_ref[rows:FIRST, :]
            out_ref[at, 104:PIECE, :] = jnp.zeros((PIECE - 104, LANES), jnp.float32)
        else:
            out_ref[at, :PIECE, :] = jnp.zeros((PIECE, LANES), jnp.float32)
        out_ref[at, PIECE:, :] = n_ref[...]


def pieces_of(e, first, second, n):
    vmem = pl.BlockSpec(memory_space=pltpu.VMEM)
    return pl.pallas_call(
        pieces_kernel,
        in_specs=[pl.BlockSpec(memory_space=pltpu.SMEM), vmem, vmem, vmem],
        out_specs=vmem,
        out_shape=pltpu.VMEM((NB, PIECE + TAIL, LANES), jnp.float32),
        scratch_shapes=[pltpu.VMEM((320, 320), jnp.float32)],
        cost_estimate=pl.CostEstimate(flops=0, bytes_accessed=1_300_000, transcendentals=0),
    )(e, first, second, n)


def tail_of(array):
    return array.reshape(-1, array.shape[-2], LANES)[0, -TAIL:, :].astype(jnp.float32)


def scales_of(arrays):
    tails = [tail_of(a) for a in arrays]
    n = tails[0]
    for tail in tails[1:]:
        n = jnp.maximum(n, tail)
    n = n + 2.0
    n, *factors = lax.optimization_barrier((n, *[power_of_two(t - n) for t in tails]))
    return n, factors


def total_of(arrays, factors):
    return sum(a.astype(jnp.float32) * f[:1] for a, f in zip(arrays, factors))


def with_tail(total, n):
    is_tail = lax.broadcasted_iota(jnp.int32, total.shape, total.ndim - 2) >= total.shape[-2] - TAIL
    return jnp.where(is_tail, n[:1], total)


def per_device(gradients, coeffs):
    rows, width = gradients.shape
    quarter, half = rows // 4, rows // 2
    e = lax.axis_index("ex")
    w = lax.axis_index("wa")
    x, y = e >> 2, e & 3
    z, h, c = w >> 2, (w >> 1) & 1, w & 1
    ring = 2 * h + x

    mine = lax.all_to_all(gradients.reshape(rows, NB, width // NB), "ex", 1, 0)
    other = moved(mine, lambda x, y, z, h, c: (x, y, z, h, 1 - c))
    column_coeffs = moved(coeffs, lambda x, y, z, h, c: (z // 4, z % 4, 4 * x + y, h, c))
    column_coeffs = lax.dynamic_slice_in_dim(column_coeffs, (w & 3) * quarter, quarter)

    most = jnp.broadcast_to(jnp.max(jnp.abs(mine)).astype(jnp.float32), (TAIL, LANES))
    most = jnp.maximum(most, moved(most, lambda x, y, z, h, c: (x, y, z, h, 1 - c)))
    bound = jnp.maximum(most * most * (2.0 * width / NB), 1e-30)
    n = jnp.ceil(jnp.log2(bound)) - 11.0
    scale = jnp.stack([n, power_of_two(-n)])

    first, second = products(jnp.reshape(c, (1,)).astype(jnp.int32), scale, mine, other)

    def for_x(array, d):
        to = (ring + d) & 3
        array = lax.dynamic_index_in_dim(array, to & 1, array.ndim - 4, keepdims=False)
        return lax.dynamic_index_in_dim(array, to >> 1, array.ndim - 3, keepdims=False)

    def for_y(array, d):
        return lax.dynamic_index_in_dim(array, (y + d) & 3, 0, keepdims=False)

    def all_along_x(array):
        return [for_x(array, 0)] + [along_x(for_x(array, d).astype(jnp.float16), d) for d in (2, 1, 3)]

    first, second = lax.optimization_barrier((first.astype(jnp.float16), second))
    first = lax.all_to_all(first, "ex", 0, 0, axis_index_groups=[[0, 1, 2, 3], [4, 5, 6, 7]])
    second_all = all_along_x(second)
    n, factors = scales_of(second_all)
    second = with_tail(total_of(second_all, factors), n)
    second_all = [for_y(second, 0)] + [along_y(for_y(second, d).astype(jnp.float16), d) for d in (2, 1, 3)]
    n, factors = scales_of([first[s] for s in range(4)])
    factors = jnp.stack([f[:1] for f in factors]).reshape(4, 1, 1, 1, LANES)
    first = with_tail(jnp.sum(first.astype(jnp.float32) * factors, 0), n)
    first_all = all_along_x(first)
    n, factors = scales_of(first_all + second_all)
    pieces = pieces_of(
        jnp.reshape(e, (1,)).astype(jnp.int32), total_of(first_all, factors[:4]), total_of(second_all, factors[4:]), n
    )

    groups = [[zz * 4 + at for zz in range(NB)] for at in range(4)]
    parts = lax.all_to_all(pieces.astype(jnp.float16), "wa", 0, 0, axis_index_groups=groups)
    factors = lax.optimization_barrier(power_of_two(parts[:, -1:, :].astype(jnp.float32)))
    final = jnp.sum(parts.astype(jnp.float32) * factors, 0)[:PIECE]

    normal = jnp.concatenate(
        [final[:80], final[80:160], jnp.concatenate([final[160:, :64], final[160:, 64:]], 0)], 1
    )
    rest = [final[80:104, 0:32], final[80:104, 32:64], final[80:104, 64:96], final[80:88, 96:]]
    kept = jnp.concatenate([final[:80], jnp.concatenate(rest, 0)], 1)
    kept = jnp.concatenate([kept, kept], 1)
    k = (z - e) & (NB - 1)
    kept_half = jnp.where(e < 4, h, 1 - h)
    final = jnp.where(k == 4, kept, normal).reshape(quarter, 4, quarter).transpose(1, 0, 2)

    def mirror_route(dh, dc):
        def route(x, y, z, h, c):
            e, k = 4 * x + y, (z - 4 * x - y) % NB
            sends = k in (1, 2, 3) or (k == 4 and dh == x)
            return (z // 4, z % 4, e, h ^ dh, c ^ dc) if sends else None

        return route

    def from_own(quarters):
        quarters = jnp.where(c == 1, jnp.stack([quarters[1], quarters[0], quarters[3], quarters[2]]), quarters)
        return jnp.where(h == 1, jnp.stack([quarters[2], quarters[3], quarters[0], quarters[1]]), quarters)

    sent = from_own(final)
    mirrored = from_own(jnp.stack([moved(sent[2 * dh + dc], mirror_route(dh, dc)) for dh in range(2) for dc in range(2)]))
    halves = jnp.arange(4)[:, None, None] // 2
    direct = (k < 4) | ((k == 4) & (halves == kept_half))
    final = jnp.where(direct, final.transpose(0, 2, 1), mirrored).reshape(rows, quarter)
    return (coeffs[:, None] * final) * column_coeffs[None, :]


def solution(mesh):
    placed = (P("ex", "wa"), P("ex"))
    return jax.shard_map(
        per_device, mesh=mesh, in_specs=placed, out_specs=P("ex", "wa"), check_vma=False
    )
```

```python
import jax
import jax.numpy as jnp
from jax import lax
from jax.experimental import pallas as pl
from jax.experimental.pallas import tpu as pltpu
from jax.sharding import PartitionSpec as P

NB = 8
LANES = 128
FIRST, SECOND, PIECE = 424, 480, 200
TAIL = 8


def moved(value, route):
    pairs = []
    for e in range(NB):
        for w in range(4 * NB):
            to = route(e // 4, e % 4, w // 4, w // 2 % 2, w % 2)
            if to is not None:
                tx, ty, tz, th, tc = to
                pairs.append(((e * 4 * NB) + w, (tx * 4 + ty) * 4 * NB + tz * 4 + th * 2 + tc))
    return lax.ppermute(value, ("ex", "wa"), pairs)


def along_y(value, d):
    return moved(value, lambda x, y, z, h, c: (x, (y + d) % 4, z, h, c))


def along_x(value, d):
    def route(x, y, z, h, c):
        to = (2 * h + x + d) % 4
        return to % 2, y, z, to // 2, c

    return moved(value, route)


def dot_nt(left, right):
    return lax.dot_general(
        left, right, (((1,), (1,)), ((), ())), preferred_element_type=jnp.float32
    )


def power_of_two(n):
    left, size = jnp.abs(n), jnp.ones_like(n)
    for bit in (64.0, 32.0, 16.0, 8.0, 4.0, 2.0, 1.0):
        has = left >= bit
        size = jnp.where(has, size * 2.0**bit, size)
        left = jnp.where(has, left - bit, left)
    return jnp.where(n < 0, 1.0 / size, size)


def products_kernel(core_ref, scale_ref, mine_ref, other_ref, first_ref, second_ref, held, columns, arrived):
    step = pl.program_id(0)
    rows, k = mine_ref.shape[1:]
    quarter, half = rows // 4, rows // 2

    def fetches(j):
        return [
            pltpu.make_async_copy(ref.at[j], held.at[j, :, pl.ds(part * k, k)], arrived.at[part, j])
            for part, ref in enumerate((mine_ref, other_ref))
        ]

    def take(j):
        for fetch in fetches(j):
            fetch.wait()
        for h in range(2):
            at = pl.ds(pl.multiple_of(h * half + core_ref[0] * quarter, quarter), quarter)
            own = held[j, at, :]
            columns[h, pl.ds(j * quarter, quarter), :] = own
            if j < 4:
                columns[h, pl.ds((j + NB) * quarter, quarter), :] = own

    @pl.when(step == 0)
    def _():
        for j in range(NB):
            for fetch in fetches(j):
                fetch.start()
        for j in range(NB):
            take(j)

    factor = scale_ref[1, 0:1, :]
    for sub in range(4):
        i = step * 4 + sub
        start = pl.multiple_of(i * quarter, quarter)
        for h in range(2):
            tile = dot_nt(held[i], columns[h, pl.ds(start, 5 * quarter), :])
            first_ref[sub, 0, h, :rows, :] = tile[:, :128] * factor
            kept = jnp.where((step == 0) == (h == 0), tile[:half, 256:], tile[half:, 256:]).T[64:]
            first_ref[sub, 0, h, rows : rows + 80, :] = kept[:, :128] * factor
            for q in range(3):
                first_ref[sub, 0, h, rows + 80 : rows + 104, 32 * q : 32 * q + 32] = (
                    kept[24 * q : 24 * q + 24, 128:] * factor[:, :32]
                )
            first_ref[sub, 0, h, rows + 80 : rows + 88, 96:] = kept[72:, 128:] * factor[:, :32]
            first_ref[sub, 0, h, rows + 88 : rows + 104, 96:] = jnp.zeros((16, 32), jnp.float32)
            first_ref[sub, 0, h, FIRST:, :] = scale_ref[0]
            second_ref[sub, 0, h, :rows, :] = tile[:, 128:256] * factor
            second_ref[sub, 0, h, rows:SECOND, :64] = tile[:half, 256:320] * factor[:, :64]
            second_ref[sub, 0, h, rows:SECOND, 64:] = tile[half:, 256:320] * factor[:, :64]
            second_ref[sub, 0, h, SECOND:, :] = scale_ref[0]


def products(core, scale, mine, other):
    _, rows, k = mine.shape
    shapes = [(4, 2, 2, FIRST + TAIL, LANES), (4, 2, 2, SECOND + TAIL, LANES)]
    anywhere = pl.BlockSpec(memory_space=pl.ANY)
    return pl.pallas_call(
        products_kernel,
        grid=(2,),
        in_specs=[
            pl.BlockSpec(memory_space=pltpu.SMEM),
            pl.BlockSpec(scale.shape, lambda i: (0, 0, 0)),
            anywhere,
            anywhere,
        ],
        out_specs=[pl.BlockSpec((4, 1) + s[2:], lambda i: (0, i, 0, 0, 0)) for s in shapes],
        out_shape=[jax.ShapeDtypeStruct(s, jnp.float32) for s in shapes],
        scratch_shapes=[
            pltpu.VMEM((NB, rows, 2 * k), jnp.bfloat16),
            pltpu.VMEM((2, 12 * rows // 4, 2 * k), jnp.bfloat16),
            pltpu.SemaphoreType.DMA((2, NB)),
        ],
        compiler_params=pltpu.CompilerParams(vmem_limit_bytes=28 * 1024 * 1024),
        cost_estimate=pl.CostEstimate(
            flops=2 * NB * 9 * rows // 4 * rows * 2 * k, bytes_accessed=NB * rows * (k * 4 + 9 * rows), transcendentals=0
        ),
    )(core, scale, mine, other)


def chunks_kernel(array_ref, out_ref, arrived):
    k = out_ref.shape[2]
    copies = [
        pltpu.make_async_copy(array_ref.at[:, pl.ds(j * k, k)], out_ref.at[j], arrived.at[j]) for j in range(NB)
    ]
    for copy in copies:
        copy.start()
    for copy in copies:
        copy.wait()


def chunks_of(array):
    rows, columns = array.shape
    return pl.pallas_call(
        chunks_kernel,
        in_specs=[pl.BlockSpec(memory_space=pl.ANY)],
        out_specs=pl.BlockSpec(memory_space=pltpu.VMEM),
        out_shape=pltpu.VMEM((NB, rows, columns // NB), array.dtype),
        scratch_shapes=[pltpu.SemaphoreType.DMA((NB,))],
        compiler_params=pltpu.CompilerParams(vmem_limit_bytes=56 * 1024 * 1024),
        cost_estimate=pl.CostEstimate(flops=0, bytes_accessed=4 * rows * columns, transcendentals=0),
    )(array)


def pieces_kernel(e_ref, first_ref, second_ref, n_ref, out_ref, tile):
    rows, half = 320, 160
    tile[0:128, :] = first_ref[:rows, :].T
    tile[128:256, :] = second_ref[:rows, :].T
    packed = second_ref[rows:SECOND, :].T
    tile[256:320, :half] = packed[:64]
    tile[256:320, half:] = packed[64:]
    for k in range(NB):
        at = (e_ref[0] + k) & (NB - 1)
        if k < 4:
            piece = tile[k * 80 : (k + 1) * 80, :]
            out_ref[at, 0:80, :] = piece[:, :128]
            out_ref[at, 80:160, :] = piece[:, 128:256]
            out_ref[at, 160:200, :64] = piece[:40, 256:]
            out_ref[at, 160:200, 64:] = piece[40:, 256:]
        elif k == 4:
            out_ref[at, :104, :] = first_ref[rows:FIRST, :]
            out_ref[at, 104:PIECE, :] = jnp.zeros((PIECE - 104, LANES), jnp.float32)
        else:
            out_ref[at, :PIECE, :] = jnp.zeros((PIECE, LANES), jnp.float32)
        out_ref[at, PIECE:, :] = n_ref[...]


def pieces_of(e, first, second, n):
    vmem = pl.BlockSpec(memory_space=pltpu.VMEM)
    return pl.pallas_call(
        pieces_kernel,
        in_specs=[pl.BlockSpec(memory_space=pltpu.SMEM), vmem, vmem, vmem],
        out_specs=vmem,
        out_shape=pltpu.VMEM((NB, PIECE + TAIL, LANES), jnp.float32),
        scratch_shapes=[pltpu.VMEM((320, 320), jnp.float32)],
        cost_estimate=pl.CostEstimate(flops=0, bytes_accessed=1_300_000, transcendentals=0),
    )(e, first, second, n)


def tail_of(array):
    return array.reshape(-1, array.shape[-2], LANES)[0, -TAIL:, :].astype(jnp.float32)


def scales_of(arrays):
    tails = [tail_of(a) for a in arrays]
    n = tails[0]
    for tail in tails[1:]:
        n = jnp.maximum(n, tail)
    n = n + 2.0
    n, *factors = lax.optimization_barrier((n, *[power_of_two(t - n) for t in tails]))
    return n, factors


def total_of(arrays, factors):
    return sum(a.astype(jnp.float32) * f[:1] for a, f in zip(arrays, factors))


def with_tail(total, n):
    is_tail = lax.broadcasted_iota(jnp.int32, total.shape, total.ndim - 2) >= total.shape[-2] - TAIL
    return jnp.where(is_tail, n[:1], total)


def per_device(gradients, coeffs):
    rows, width = gradients.shape
    quarter, half = rows // 4, rows // 2
    e = lax.axis_index("ex")
    w = lax.axis_index("wa")
    x, y = e >> 2, e & 3
    z, h, c = w >> 2, (w >> 1) & 1, w & 1
    ring = 2 * h + x

    mine = lax.all_to_all(chunks_of(gradients), "ex", 0, 0)
    other = moved(mine, lambda x, y, z, h, c: (x, y, z, h, 1 - c))
    column_coeffs = moved(coeffs, lambda x, y, z, h, c: (z // 4, z % 4, 4 * x + y, h, c))
    column_coeffs = lax.dynamic_slice_in_dim(column_coeffs, (w & 3) * quarter, quarter)

    most = jnp.broadcast_to(jnp.max(jnp.abs(mine)).astype(jnp.float32), (TAIL, LANES))
    most = jnp.maximum(most, moved(most, lambda x, y, z, h, c: (x, y, z, h, 1 - c)))
    bound = jnp.maximum(most * most * (2.0 * width / NB), 1e-30)
    n = jnp.ceil(jnp.log2(bound)) - 11.0
    scale = jnp.stack([n, power_of_two(-n)])

    first, second = products(jnp.reshape(c, (1,)).astype(jnp.int32), scale, mine, other)

    def for_x(array, d):
        to = (ring + d) & 3
        array = lax.dynamic_index_in_dim(array, to & 1, array.ndim - 4, keepdims=False)
        return lax.dynamic_index_in_dim(array, to >> 1, array.ndim - 3, keepdims=False)

    def for_y(array, d):
        return lax.dynamic_index_in_dim(array, (y + d) & 3, 0, keepdims=False)

    def all_along_x(array):
        return [for_x(array, 0)] + [along_x(for_x(array, d).astype(jnp.float16), d) for d in (2, 1, 3)]

    first, second = lax.optimization_barrier((first.astype(jnp.float16), second))
    first = lax.all_to_all(first, "ex", 0, 0, axis_index_groups=[[0, 1, 2, 3], [4, 5, 6, 7]])
    second_all = all_along_x(second)
    n, factors = scales_of(second_all)
    second = with_tail(total_of(second_all, factors), n)
    second_all = [for_y(second, 0)] + [along_y(for_y(second, d).astype(jnp.float16), d) for d in (2, 1, 3)]
    n, factors = scales_of([first[s] for s in range(4)])
    factors = jnp.stack([f[:1] for f in factors]).reshape(4, 1, 1, 1, LANES)
    first = with_tail(jnp.sum(first.astype(jnp.float32) * factors, 0), n)
    first_all = all_along_x(first)
    n, factors = scales_of(first_all + second_all)
    pieces = pieces_of(
        jnp.reshape(e, (1,)).astype(jnp.int32), total_of(first_all, factors[:4]), total_of(second_all, factors[4:]), n
    )

    groups = [[zz * 4 + at for zz in range(NB)] for at in range(4)]
    parts = lax.all_to_all(pieces.astype(jnp.float16), "wa", 0, 0, axis_index_groups=groups)
    factors = lax.optimization_barrier(power_of_two(parts[:, -1:, :].astype(jnp.float32)))
    final = jnp.sum(parts.astype(jnp.float32) * factors, 0)[:PIECE]

    normal = jnp.concatenate(
        [final[:80], final[80:160], jnp.concatenate([final[160:, :64], final[160:, 64:]], 0)], 1
    )
    rest = [final[80:104, 0:32], final[80:104, 32:64], final[80:104, 64:96], final[80:88, 96:]]
    kept = jnp.concatenate([final[:80], jnp.concatenate(rest, 0)], 1)
    kept = jnp.concatenate([kept, kept], 1)
    k = (z - e) & (NB - 1)
    kept_half = jnp.where(e < 4, h, 1 - h)
    final = jnp.where(k == 4, kept, normal).reshape(quarter, 4, quarter).transpose(1, 0, 2)

    def mirror_route(dh, dc):
        def route(x, y, z, h, c):
            e, k = 4 * x + y, (z - 4 * x - y) % NB
            sends = k in (1, 2, 3) or (k == 4 and dh == x)
            return (z // 4, z % 4, e, h ^ dh, c ^ dc) if sends else None

        return route

    def from_own(quarters):
        quarters = jnp.where(c == 1, jnp.stack([quarters[1], quarters[0], quarters[3], quarters[2]]), quarters)
        return jnp.where(h == 1, jnp.stack([quarters[2], quarters[3], quarters[0], quarters[1]]), quarters)

    sent = from_own(final)
    mirrored = from_own(jnp.stack([moved(sent[2 * dh + dc], mirror_route(dh, dc)) for dh in range(2) for dc in range(2)]))
    halves = jnp.arange(4)[:, None, None] // 2
    direct = (k < 4) | ((k == 4) & (halves == kept_half))
    final = jnp.where(direct, final.transpose(0, 2, 1), mirrored).reshape(rows, quarter)
    return (coeffs[:, None] * final) * column_coeffs[None, :]


def solution(mesh):
    placed = (P("ex", "wa"), P("ex"))
    return jax.shard_map(
        per_device, mesh=mesh, in_specs=placed, out_specs=P("ex", "wa"), check_vma=False
    )
```

```python
import jax
import jax.numpy as jnp
from jax import lax
from jax.experimental import pallas as pl
from jax.experimental.pallas import tpu as pltpu
from jax.sharding import PartitionSpec as P

NB = 8
LANES = 128
FIRST, SECOND, PIECE = 424, 480, 200
TAIL = 8


def moved(value, route):
    pairs = []
    for e in range(NB):
        for w in range(4 * NB):
            to = route(e // 4, e % 4, w // 4, w // 2 % 2, w % 2)
            if to is not None:
                tx, ty, tz, th, tc = to
                pairs.append(((e * 4 * NB) + w, (tx * 4 + ty) * 4 * NB + tz * 4 + th * 2 + tc))
    return lax.ppermute(value, ("ex", "wa"), pairs)


def along_y(value, d):
    return moved(value, lambda x, y, z, h, c: (x, (y + d) % 4, z, h, c))


def along_x(value, d):
    def route(x, y, z, h, c):
        to = (2 * h + x + d) % 4
        return to % 2, y, z, to // 2, c

    return moved(value, route)


def dot_nt(left, right):
    return lax.dot_general(
        left, right, (((1,), (1,)), ((), ())), preferred_element_type=jnp.float32
    )


def power_of_two(n):
    left, size = jnp.abs(n), jnp.ones_like(n)
    for bit in (64.0, 32.0, 16.0, 8.0, 4.0, 2.0, 1.0):
        has = left >= bit
        size = jnp.where(has, size * 2.0**bit, size)
        left = jnp.where(has, left - bit, left)
    return jnp.where(n < 0, 1.0 / size, size)


def products_kernel(core_ref, scale_ref, mine_ref, other_ref, first_ref, second_ref, held, columns, arrived):
    step = pl.program_id(0)
    rows, k = mine_ref.shape[1:]
    quarter, half = rows // 4, rows // 2

    def fetches(j):
        return [
            pltpu.make_async_copy(ref.at[j], held.at[j, :, pl.ds(part * k, k)], arrived.at[part, j])
            for part, ref in enumerate((mine_ref, other_ref))
        ]

    def take(j):
        for fetch in fetches(j):
            fetch.wait()
        for h in range(2):
            at = pl.ds(pl.multiple_of(h * half + core_ref[0] * quarter, quarter), quarter)
            own = held[j, at, :]
            columns[h, pl.ds(j * quarter, quarter), :] = own
            if j < 4:
                columns[h, pl.ds((j + NB) * quarter, quarter), :] = own

    @pl.when(step == 0)
    def _():
        for j in range(NB):
            for fetch in fetches(j):
                fetch.start()
        for j in range(NB):
            take(j)

    factor = scale_ref[1, 0:1, :]
    for sub in range(4):
        i = step * 4 + sub
        start = pl.multiple_of(i * quarter, quarter)
        for h in range(2):
            tile = dot_nt(held[i], columns[h, pl.ds(start, 5 * quarter), :])
            first_ref[sub, 0, h, :rows, :] = tile[:, :128] * factor
            kept = jnp.where((step == 0) == (h == 0), tile[:half, 256:], tile[half:, 256:]).T[64:]
            first_ref[sub, 0, h, rows : rows + 80, :] = kept[:, :128] * factor
            for q in range(3):
                first_ref[sub, 0, h, rows + 80 : rows + 104, 32 * q : 32 * q + 32] = (
                    kept[24 * q : 24 * q + 24, 128:] * factor[:, :32]
                )
            first_ref[sub, 0, h, rows + 80 : rows + 88, 96:] = kept[72:, 128:] * factor[:, :32]
            first_ref[sub, 0, h, rows + 88 : rows + 104, 96:] = jnp.zeros((16, 32), jnp.float32)
            first_ref[sub, 0, h, FIRST:, :] = scale_ref[0]
            second_ref[sub, 0, h, :rows, :] = tile[:, 128:256] * factor
            second_ref[sub, 0, h, rows:SECOND, :64] = tile[:half, 256:320] * factor[:, :64]
            second_ref[sub, 0, h, rows:SECOND, 64:] = tile[half:, 256:320] * factor[:, :64]
            second_ref[sub, 0, h, SECOND:, :] = scale_ref[0]


def products(core, scale, mine, other):
    _, rows, k = mine.shape
    shapes = [(4, 2, 2, FIRST + TAIL, LANES), (4, 2, 2, SECOND + TAIL, LANES)]
    anywhere = pl.BlockSpec(memory_space=pl.ANY)
    return pl.pallas_call(
        products_kernel,
        grid=(2,),
        in_specs=[
            pl.BlockSpec(memory_space=pltpu.SMEM),
            pl.BlockSpec(scale.shape, lambda i: (0, 0, 0)),
            anywhere,
            anywhere,
        ],
        out_specs=[pl.BlockSpec((4, 1) + s[2:], lambda i: (0, i, 0, 0, 0)) for s in shapes],
        out_shape=[jax.ShapeDtypeStruct(s, jnp.float32) for s in shapes],
        scratch_shapes=[
            pltpu.VMEM((NB, rows, 2 * k), jnp.bfloat16),
            pltpu.VMEM((2, 12 * rows // 4, 2 * k), jnp.bfloat16),
            pltpu.SemaphoreType.DMA((2, NB)),
        ],
        compiler_params=pltpu.CompilerParams(vmem_limit_bytes=28 * 1024 * 1024),
        cost_estimate=pl.CostEstimate(
            flops=2 * NB * 9 * rows // 4 * rows * 2 * k, bytes_accessed=NB * rows * (k * 4 + 9 * rows), transcendentals=0
        ),
    )(core, scale, mine, other)


def chunks_kernel(array_ref, out_ref, arrived):
    k = out_ref.shape[2]
    copies = [
        pltpu.make_async_copy(array_ref.at[:, pl.ds(j * k, k)], out_ref.at[j], arrived.at[j]) for j in range(NB)
    ]
    for copy in copies:
        copy.start()
    for copy in copies:
        copy.wait()


def chunks_of(array):
    rows, columns = array.shape
    return pl.pallas_call(
        chunks_kernel,
        in_specs=[pl.BlockSpec(memory_space=pl.ANY)],
        out_specs=pl.BlockSpec(memory_space=pltpu.VMEM),
        out_shape=pltpu.VMEM((NB, rows, columns // NB), array.dtype),
        scratch_shapes=[pltpu.SemaphoreType.DMA((NB,))],
        compiler_params=pltpu.CompilerParams(vmem_limit_bytes=56 * 1024 * 1024),
        cost_estimate=pl.CostEstimate(flops=0, bytes_accessed=4 * rows * columns, transcendentals=0),
    )(array)


def pieces_kernel(e_ref, first_ref, second_ref, n_ref, out_ref, tile):
    rows, half = 320, 160
    tile[0:128, :] = first_ref[:rows, :].T
    tile[128:256, :] = second_ref[:rows, :].T
    packed = second_ref[rows:SECOND, :].T
    tile[256:320, :half] = packed[:64]
    tile[256:320, half:] = packed[64:]
    for k in range(NB):
        at = (e_ref[0] + k) & (NB - 1)
        if k < 4:
            piece = tile[k * 80 : (k + 1) * 80, :]
            out_ref[at, 0:80, :] = piece[:, :128]
            out_ref[at, 80:160, :] = piece[:, 128:256]
            out_ref[at, 160:200, :64] = piece[:40, 256:]
            out_ref[at, 160:200, 64:] = piece[40:, 256:]
        elif k == 4:
            out_ref[at, :104, :] = first_ref[rows:FIRST, :]
            out_ref[at, 104:PIECE, :] = jnp.zeros((PIECE - 104, LANES), jnp.float32)
        else:
            out_ref[at, :PIECE, :] = jnp.zeros((PIECE, LANES), jnp.float32)
        out_ref[at, PIECE:, :] = n_ref[...]


def pieces_of(e, first, second, n):
    vmem = pl.BlockSpec(memory_space=pltpu.VMEM)
    return pl.pallas_call(
        pieces_kernel,
        in_specs=[pl.BlockSpec(memory_space=pltpu.SMEM), vmem, vmem, vmem],
        out_specs=vmem,
        out_shape=pltpu.VMEM((NB, PIECE + TAIL, LANES), jnp.float32),
        scratch_shapes=[pltpu.VMEM((320, 320), jnp.float32)],
        cost_estimate=pl.CostEstimate(flops=0, bytes_accessed=1_300_000, transcendentals=0),
    )(e, first, second, n)


def decode_kernel(place_ref, total_ref, direct_ref, sent_ref):
    own, opposite = place_ref[0], place_ref[1]

    @pl.when(opposite == 0)
    def _():
        direct_ref[:, :128] = total_ref[:80, :]
        direct_ref[:, 128:256] = total_ref[80:160, :]
        direct_ref[:40, 256:] = total_ref[160:200, :64]
        direct_ref[40:, 256:] = total_ref[160:200, 64:]

    @pl.when(opposite != 0)
    def _():
        for start in (0, 160):
            direct_ref[:, start : start + 128] = total_ref[:80, :]
            for q in range(3):
                direct_ref[24 * q : 24 * q + 24, start + 128 : start + 160] = total_ref[80:104, 32 * q : 32 * q + 32]
            direct_ref[72:, start + 128 : start + 160] = total_ref[80:88, 96:]

    turned = direct_ref[...].T
    for b in range(4):
        piece = turned[b * 80 : b * 80 + 80]
        to = own ^ b
        sent_ref[to, :40, :64] = piece[:40, :64]
        sent_ref[to, :40, 64:] = piece[40:, :64]
        for g in range(5):
            sent_ref[to, 40:, 16 * g : 16 * g + 16] = piece[16 * g : 16 * g + 16, 64:]
        sent_ref[to, 40:, 80:] = jnp.zeros((16, 48), jnp.float32)


def decoded(place, total):
    vmem = pl.BlockSpec(memory_space=pltpu.VMEM)
    return pl.pallas_call(
        decode_kernel,
        in_specs=[pl.BlockSpec(memory_space=pltpu.SMEM), vmem],
        out_specs=[vmem, vmem],
        out_shape=[jax.ShapeDtypeStruct((80, 320), jnp.float32), jax.ShapeDtypeStruct((4, 56, LANES), jnp.float32)],
        cost_estimate=pl.CostEstimate(flops=0, bytes_accessed=400_000, transcendentals=0),
    )(place, total)


def assemble_kernel(place_ref, direct_ref, m0, m1, m2, m3, rows_ref, columns_ref, out_ref, mirrored):
    own, opposite, none, kept_half = place_ref[0], place_ref[1], place_ref[2], place_ref[3]
    for d, got in enumerate((m0, m1, m2, m3)):
        at = own ^ d
        mirrored[at, :40, :64] = got[:40, :64]
        mirrored[at, 40:, :64] = got[:40, 64:]
        for g in range(5):
            mirrored[at, 16 * g : 16 * g + 16, 64:] = got[40:, 16 * g : 16 * g + 16]
    for b in range(4):
        lanes = slice(b * 80, b * 80 + 80)
        takes = (none != 0) | ((opposite != 0) & (kept_half != b // 2))
        value = jnp.where(takes, mirrored[b], direct_ref[:, lanes])
        out_ref[:, lanes] = rows_ref[:, lanes] * value * columns_ref[:, :80]


def assembled(place, direct, pieces, row_coeffs, column_coeffs):
    vmem = pl.BlockSpec(memory_space=pltpu.VMEM)
    return pl.pallas_call(
        assemble_kernel,
        in_specs=[pl.BlockSpec(memory_space=pltpu.SMEM)] + [vmem] * 7,
        out_specs=vmem,
        out_shape=jax.ShapeDtypeStruct((80, 320), jnp.float32),
        scratch_shapes=[pltpu.VMEM((4, 80, 80), jnp.float32)],
        cost_estimate=pl.CostEstimate(flops=60_000, bytes_accessed=500_000, transcendentals=0),
    )(place, direct, *pieces, row_coeffs, column_coeffs)


def tail_of(array):
    return array.reshape(-1, array.shape[-2], LANES)[0, -TAIL:, :].astype(jnp.float32)


def scales_of(arrays):
    tails = [tail_of(a) for a in arrays]
    n = tails[0]
    for tail in tails[1:]:
        n = jnp.maximum(n, tail)
    n = n + 2.0
    n, *factors = lax.optimization_barrier((n, *[power_of_two(t - n) for t in tails]))
    return n, factors


def total_of(arrays, factors):
    return sum(a.astype(jnp.float32) * f[:1] for a, f in zip(arrays, factors))


def with_tail(total, n):
    is_tail = lax.broadcasted_iota(jnp.int32, total.shape, total.ndim - 2) >= total.shape[-2] - TAIL
    return jnp.where(is_tail, n[:1], total)


def per_device(gradients, coeffs):
    rows, width = gradients.shape
    quarter, half = rows // 4, rows // 2
    e = lax.axis_index("ex")
    w = lax.axis_index("wa")
    x, y = e >> 2, e & 3
    z, h, c = w >> 2, (w >> 1) & 1, w & 1
    ring = 2 * h + x

    mine = lax.all_to_all(chunks_of(gradients), "ex", 0, 0)
    other = moved(mine, lambda x, y, z, h, c: (x, y, z, h, 1 - c))
    column_coeffs = moved(coeffs, lambda x, y, z, h, c: (z // 4, z % 4, 4 * x + y, h, c))
    column_coeffs = lax.dynamic_slice_in_dim(column_coeffs, (w & 3) * quarter, quarter)

    most = jnp.broadcast_to(jnp.max(jnp.abs(mine)).astype(jnp.float32), (TAIL, LANES))
    most = jnp.maximum(most, moved(most, lambda x, y, z, h, c: (x, y, z, h, 1 - c)))
    bound = jnp.maximum(most * most * (2.0 * width / NB), 1e-30)
    n = jnp.ceil(jnp.log2(bound)) - 11.0
    scale = jnp.stack([n, power_of_two(-n)])

    first, second = products(jnp.reshape(c, (1,)).astype(jnp.int32), scale, mine, other)

    def for_x(array, d):
        to = (ring + d) & 3
        array = lax.dynamic_index_in_dim(array, to & 1, array.ndim - 4, keepdims=False)
        return lax.dynamic_index_in_dim(array, to >> 1, array.ndim - 3, keepdims=False)

    def for_y(array, d):
        return lax.dynamic_index_in_dim(array, (y + d) & 3, 0, keepdims=False)

    def all_along_x(array):
        return [for_x(array, 0)] + [along_x(for_x(array, d).astype(jnp.float16), d) for d in (2, 1, 3)]

    first, second = lax.optimization_barrier((first.astype(jnp.float16), second))
    first = lax.all_to_all(first, "ex", 0, 0, axis_index_groups=[[0, 1, 2, 3], [4, 5, 6, 7]])
    second_all = all_along_x(second)
    n, factors = scales_of(second_all)
    second = with_tail(total_of(second_all, factors), n)
    second_all = [for_y(second, 0)] + [along_y(for_y(second, d).astype(jnp.float16), d) for d in (2, 1, 3)]
    n, factors = scales_of([first[s] for s in range(4)])
    factors = jnp.stack([f[:1] for f in factors]).reshape(4, 1, 1, 1, LANES)
    first = with_tail(jnp.sum(first.astype(jnp.float32) * factors, 0), n)
    first_all = all_along_x(first)
    n, factors = scales_of(first_all + second_all)
    pieces = pieces_of(
        jnp.reshape(e, (1,)).astype(jnp.int32), total_of(first_all, factors[:4]), total_of(second_all, factors[4:]), n
    )

    groups = [[zz * 4 + at for zz in range(NB)] for at in range(4)]
    parts = lax.all_to_all(pieces.astype(jnp.float16), "wa", 0, 0, axis_index_groups=groups)
    factors = lax.optimization_barrier(power_of_two(parts[:, -1:, :].astype(jnp.float32)))
    total = jnp.sum(parts.astype(jnp.float32) * factors, 0)

    k = (z - e) & (NB - 1)
    kept_half = jnp.where(e < 4, h, 1 - h)
    place = jnp.stack([w & 3, (k == 4).astype(jnp.int32), (k > 4).astype(jnp.int32), kept_half]).astype(jnp.int32)
    direct, sent = decoded(place, total)

    def mirror_route(dh, dc):
        def route(x, y, z, h, c):
            e, k = 4 * x + y, (z - 4 * x - y) % NB
            sends = k in (1, 2, 3) or (k == 4 and dh == x)
            return (z // 4, z % 4, e, h ^ dh, c ^ dc) if sends else None

        return route

    pieces = [moved(sent[2 * dh + dc], mirror_route(dh, dc)) for dh in range(2) for dc in range(2)]
    column_coeffs = jnp.broadcast_to(column_coeffs[:, None], (quarter, LANES))
    return assembled(place, direct, pieces, coeffs[None, :], column_coeffs).T


def solution(mesh):
    placed = (P("ex", "wa"), P("ex"))
    return jax.shard_map(
        per_device, mesh=mesh, in_specs=placed, out_specs=P("ex", "wa"), check_vma=False
    )
```

```python
import jax
import jax.numpy as jnp
from jax import lax
from jax.experimental import pallas as pl
from jax.experimental.pallas import tpu as pltpu
from jax.sharding import PartitionSpec as P

NB = 8
LANES = 128
FIRST, SECOND, PIECE = 424, 480, 200
TAIL = 8


def moved(value, route):
    pairs = []
    for e in range(NB):
        for w in range(4 * NB):
            to = route(e // 4, e % 4, w // 4, w // 2 % 2, w % 2)
            if to is not None:
                tx, ty, tz, th, tc = to
                pairs.append(((e * 4 * NB) + w, (tx * 4 + ty) * 4 * NB + tz * 4 + th * 2 + tc))
    return lax.ppermute(value, ("ex", "wa"), pairs)


def along_y(value, d):
    return moved(value, lambda x, y, z, h, c: (x, (y + d) % 4, z, h, c))


def along_x(value, d):
    def route(x, y, z, h, c):
        to = (2 * h + x + d) % 4
        return to % 2, y, z, to // 2, c

    return moved(value, route)


def dot_nt(left, right):
    return lax.dot_general(
        left, right, (((1,), (1,)), ((), ())), preferred_element_type=jnp.float32
    )


def power_of_two(n):
    left, size = jnp.abs(n), jnp.ones_like(n)
    for bit in (64.0, 32.0, 16.0, 8.0, 4.0, 2.0, 1.0):
        has = left >= bit
        size = jnp.where(has, size * 2.0**bit, size)
        left = jnp.where(has, left - bit, left)
    return jnp.where(n < 0, 1.0 / size, size)


def products_kernel(core_ref, scale_ref, mine_ref, other_ref, first_ref, second_ref, held, columns, arrived):
    step = pl.program_id(0)
    rows, k = mine_ref.shape[1:]
    quarter, half = rows // 4, rows // 2

    def fetches(j):
        return [
            pltpu.make_async_copy(ref.at[j], held.at[j, :, pl.ds(part * k, k)], arrived.at[part, j])
            for part, ref in enumerate((mine_ref, other_ref))
        ]

    def take(j):
        for fetch in fetches(j):
            fetch.wait()
        for h in range(2):
            at = pl.ds(pl.multiple_of(h * half + core_ref[0] * quarter, quarter), quarter)
            own = held[j, at, :]
            columns[h, pl.ds(j * quarter, quarter), :] = own
            if j < 4:
                columns[h, pl.ds((j + NB) * quarter, quarter), :] = own

    @pl.when(step == 0)
    def _():
        for j in range(NB):
            for fetch in fetches(j):
                fetch.start()
        for j in range(NB):
            take(j)

    factor = scale_ref[1, 0:1, :]
    for sub in range(4):
        i = step * 4 + sub
        start = pl.multiple_of(i * quarter, quarter)
        for h in range(2):
            tile = dot_nt(held[i], columns[h, pl.ds(start, 5 * quarter), :])
            first_ref[sub, 0, h, :rows, :] = tile[:, :128] * factor
            kept = jnp.where((step == 0) == (h == 0), tile[:half, 256:], tile[half:, 256:]).T[64:]
            first_ref[sub, 0, h, rows : rows + 80, :] = kept[:, :128] * factor
            for q in range(3):
                first_ref[sub, 0, h, rows + 80 : rows + 104, 32 * q : 32 * q + 32] = (
                    kept[24 * q : 24 * q + 24, 128:] * factor[:, :32]
                )
            first_ref[sub, 0, h, rows + 80 : rows + 88, 96:] = kept[72:, 128:] * factor[:, :32]
            first_ref[sub, 0, h, rows + 88 : rows + 104, 96:] = jnp.zeros((16, 32), jnp.float32)
            first_ref[sub, 0, h, FIRST:, :] = scale_ref[0]
            second_ref[sub, 0, h, :rows, :] = tile[:, 128:256] * factor
            second_ref[sub, 0, h, rows:SECOND, :64] = tile[:half, 256:320] * factor[:, :64]
            second_ref[sub, 0, h, rows:SECOND, 64:] = tile[half:, 256:320] * factor[:, :64]
            second_ref[sub, 0, h, SECOND:, :] = scale_ref[0]


def products(core, scale, mine, other):
    _, rows, k = mine.shape
    shapes = [(4, 2, 2, FIRST + TAIL, LANES), (4, 2, 2, SECOND + TAIL, LANES)]
    anywhere = pl.BlockSpec(memory_space=pl.ANY)
    return pl.pallas_call(
        products_kernel,
        grid=(2,),
        in_specs=[
            pl.BlockSpec(memory_space=pltpu.SMEM),
            pl.BlockSpec(scale.shape, lambda i: (0, 0, 0)),
            anywhere,
            anywhere,
        ],
        out_specs=[pl.BlockSpec((4, 1) + s[2:], lambda i: (0, i, 0, 0, 0)) for s in shapes],
        out_shape=[jax.ShapeDtypeStruct(s, jnp.float32) for s in shapes],
        scratch_shapes=[
            pltpu.VMEM((NB, rows, 2 * k), jnp.bfloat16),
            pltpu.VMEM((2, 12 * rows // 4, 2 * k), jnp.bfloat16),
            pltpu.SemaphoreType.DMA((2, NB)),
        ],
        compiler_params=pltpu.CompilerParams(vmem_limit_bytes=28 * 1024 * 1024),
        cost_estimate=pl.CostEstimate(
            flops=2 * NB * 9 * rows // 4 * rows * 2 * k, bytes_accessed=NB * rows * (k * 4 + 9 * rows), transcendentals=0
        ),
    )(core, scale, mine, other)


def chunks_kernel(array_ref, out_ref, arrived):
    k = out_ref.shape[2]
    copies = [
        pltpu.make_async_copy(array_ref.at[:, pl.ds(j * k, k)], out_ref.at[j], arrived.at[j]) for j in range(NB)
    ]
    for copy in copies:
        copy.start()
    for copy in copies:
        copy.wait()


def chunks_of(array):
    rows, columns = array.shape
    return pl.pallas_call(
        chunks_kernel,
        in_specs=[pl.BlockSpec(memory_space=pl.ANY)],
        out_specs=pl.BlockSpec(memory_space=pltpu.VMEM),
        out_shape=pltpu.VMEM((NB, rows, columns // NB), array.dtype),
        scratch_shapes=[pltpu.SemaphoreType.DMA((NB,))],
        compiler_params=pltpu.CompilerParams(vmem_limit_bytes=56 * 1024 * 1024),
        cost_estimate=pl.CostEstimate(flops=0, bytes_accessed=4 * rows * columns, transcendentals=0),
    )(array)


def pieces_kernel(e_ref, first_ref, second_ref, n_ref, out_ref, tile):
    rows, half = 320, 160
    tile[0:128, :] = first_ref[:rows, :].T
    tile[128:256, :] = second_ref[:rows, :].T
    packed = second_ref[rows:SECOND, :].T
    tile[256:320, :half] = packed[:64]
    tile[256:320, half:] = packed[64:]
    for k in range(NB):
        at = (e_ref[0] + k) & (NB - 1)
        if k < 4:
            piece = tile[k * 80 : (k + 1) * 80, :]
            out_ref[at, 0:80, :] = piece[:, :128]
            out_ref[at, 80:160, :] = piece[:, 128:256]
            out_ref[at, 160:200, :64] = piece[:40, 256:]
            out_ref[at, 160:200, 64:] = piece[40:, 256:]
        elif k == 4:
            out_ref[at, :104, :] = first_ref[rows:FIRST, :]
            out_ref[at, 104:PIECE, :] = jnp.zeros((PIECE - 104, LANES), jnp.float32)
        else:
            out_ref[at, :PIECE, :] = jnp.zeros((PIECE, LANES), jnp.float32)
        out_ref[at, PIECE:, :] = n_ref[...]


def pieces_of(e, first, second, n):
    vmem = pl.BlockSpec(memory_space=pltpu.VMEM)
    return pl.pallas_call(
        pieces_kernel,
        in_specs=[pl.BlockSpec(memory_space=pltpu.SMEM), vmem, vmem, vmem],
        out_specs=vmem,
        out_shape=pltpu.VMEM((NB, PIECE + TAIL, LANES), jnp.float32),
        scratch_shapes=[pltpu.VMEM((320, 320), jnp.float32)],
        cost_estimate=pl.CostEstimate(flops=0, bytes_accessed=1_300_000, transcendentals=0),
    )(e, first, second, n)


def decode_kernel(place_ref, total_ref, direct_ref, s0, s1, s2, s3, turned):
    own, opposite = place_ref[0], place_ref[1]

    @pl.when(opposite == 0)
    def _():
        direct_ref[:, :128] = total_ref[:80, :]
        direct_ref[:, 128:256] = total_ref[80:160, :]
        direct_ref[:40, 256:] = total_ref[160:200, :64]
        direct_ref[40:, 256:] = total_ref[160:200, 64:]

    @pl.when(opposite != 0)
    def _():
        for start in (0, 160):
            direct_ref[:, start : start + 128] = total_ref[:80, :]
            for q in range(3):
                direct_ref[24 * q : 24 * q + 24, start + 128 : start + 160] = total_ref[80:104, 32 * q : 32 * q + 32]
            direct_ref[72:, start + 128 : start + 160] = total_ref[80:88, 96:]

    turned[...] = direct_ref[...].T
    for d, sent_ref in enumerate((s0, s1, s2, s3)):
        piece = turned[pl.ds(pl.multiple_of((own ^ d) * 80, 80), 80), :]
        sent_ref[:40, :64] = piece[:40, :64]
        sent_ref[:40, 64:] = piece[40:, :64]
        for g in range(5):
            sent_ref[40:, 16 * g : 16 * g + 16] = piece[16 * g : 16 * g + 16, 64:]
        sent_ref[40:, 80:] = jnp.zeros((16, 48), jnp.float32)


def decoded(place, total):
    vmem = pl.BlockSpec(memory_space=pltpu.VMEM)
    return pl.pallas_call(
        decode_kernel,
        in_specs=[pl.BlockSpec(memory_space=pltpu.SMEM), vmem],
        out_specs=[vmem] * 5,
        out_shape=[jax.ShapeDtypeStruct(s, jnp.float32) for s in [(80, 320)] + [(56, LANES)] * 4],
        scratch_shapes=[pltpu.VMEM((320, 80), jnp.float32)],
        cost_estimate=pl.CostEstimate(flops=0, bytes_accessed=400_000, transcendentals=0),
    )(place, total)


def assemble_kernel(place_ref, direct_ref, m0, m1, m2, m3, rows_ref, columns_ref, out_ref, mirrored):
    own, opposite, none, kept_half = place_ref[0], place_ref[1], place_ref[2], place_ref[3]
    for d, got in enumerate((m0, m1, m2, m3)):
        at = own ^ d
        mirrored[at, :40, :64] = got[:40, :64]
        mirrored[at, 40:, :64] = got[:40, 64:]
        for g in range(5):
            mirrored[at, 16 * g : 16 * g + 16, 64:] = got[40:, 16 * g : 16 * g + 16]
    for b in range(4):
        lanes = slice(b * 80, b * 80 + 80)
        takes = (none != 0) | ((opposite != 0) & (kept_half != b // 2))
        value = jnp.where(takes, mirrored[b], direct_ref[:, lanes])
        out_ref[:, lanes] = rows_ref[:, lanes] * value * columns_ref[:, :80]


def assembled(place, direct, pieces, row_coeffs, column_coeffs):
    vmem = pl.BlockSpec(memory_space=pltpu.VMEM)
    return pl.pallas_call(
        assemble_kernel,
        in_specs=[pl.BlockSpec(memory_space=pltpu.SMEM)] + [vmem] * 7,
        out_specs=vmem,
        out_shape=jax.ShapeDtypeStruct((80, 320), jnp.float32),
        scratch_shapes=[pltpu.VMEM((4, 80, 80), jnp.float32)],
        cost_estimate=pl.CostEstimate(flops=60_000, bytes_accessed=500_000, transcendentals=0),
    )(place, direct, *pieces, row_coeffs, column_coeffs)


def tail_of(array):
    return array.reshape(-1, array.shape[-2], LANES)[0, -TAIL:, :].astype(jnp.float32)


def scales_of(arrays):
    tails = [tail_of(a) for a in arrays]
    n = tails[0]
    for tail in tails[1:]:
        n = jnp.maximum(n, tail)
    n = n + 2.0
    n, *factors = lax.optimization_barrier((n, *[power_of_two(t - n) for t in tails]))
    return n, factors


def total_of(arrays, factors):
    return sum(a.astype(jnp.float32) * f[:1] for a, f in zip(arrays, factors))


def with_tail(total, n):
    is_tail = lax.broadcasted_iota(jnp.int32, total.shape, total.ndim - 2) >= total.shape[-2] - TAIL
    return jnp.where(is_tail, n[:1], total)


def per_device(gradients, coeffs):
    rows, width = gradients.shape
    quarter, half = rows // 4, rows // 2
    e = lax.axis_index("ex")
    w = lax.axis_index("wa")
    x, y = e >> 2, e & 3
    z, h, c = w >> 2, (w >> 1) & 1, w & 1
    ring = 2 * h + x

    mine = lax.all_to_all(chunks_of(gradients), "ex", 0, 0)
    other = moved(mine, lambda x, y, z, h, c: (x, y, z, h, 1 - c))
    column_coeffs = moved(coeffs, lambda x, y, z, h, c: (z // 4, z % 4, 4 * x + y, h, c))
    column_coeffs = lax.dynamic_slice_in_dim(column_coeffs, (w & 3) * quarter, quarter)
    column_coeffs = jnp.broadcast_to(column_coeffs[:, None], (quarter, LANES))

    most = jnp.broadcast_to(jnp.max(jnp.abs(mine)).astype(jnp.float32), (TAIL, LANES))
    most = jnp.maximum(most, moved(most, lambda x, y, z, h, c: (x, y, z, h, 1 - c)))
    bound = jnp.maximum(most * most * (2.0 * width / NB), 1e-30)
    n = jnp.ceil(jnp.log2(bound)) - 11.0
    scale = jnp.stack([n, power_of_two(-n)])
    scale, column_coeffs = lax.optimization_barrier((scale, column_coeffs))

    first, second = products(jnp.reshape(c, (1,)).astype(jnp.int32), scale, mine, other)

    def for_x(array, d):
        to = (ring + d) & 3
        array = lax.dynamic_index_in_dim(array, to & 1, array.ndim - 4, keepdims=False)
        return lax.dynamic_index_in_dim(array, to >> 1, array.ndim - 3, keepdims=False)

    def for_y(array, d):
        return lax.dynamic_index_in_dim(array, (y + d) & 3, 0, keepdims=False)

    def all_along_x(array):
        return [for_x(array, 0)] + [along_x(for_x(array, d).astype(jnp.float16), d) for d in (2, 1, 3)]

    first, second = lax.optimization_barrier((first.astype(jnp.float16), second))
    first = lax.all_to_all(first, "ex", 0, 0, axis_index_groups=[[0, 1, 2, 3], [4, 5, 6, 7]])
    second_all = all_along_x(second)
    n, factors = scales_of(second_all)
    second = with_tail(total_of(second_all, factors), n)
    second_all = [for_y(second, 0)] + [along_y(for_y(second, d).astype(jnp.float16), d) for d in (2, 1, 3)]
    n, factors = scales_of([first[s] for s in range(4)])
    factors = jnp.stack([f[:1] for f in factors]).reshape(4, 1, 1, 1, LANES)
    first = with_tail(jnp.sum(first.astype(jnp.float32) * factors, 0), n)
    first_all = all_along_x(first)
    n, factors = scales_of(first_all + second_all)
    pieces = pieces_of(
        jnp.reshape(e, (1,)).astype(jnp.int32), total_of(first_all, factors[:4]), total_of(second_all, factors[4:]), n
    )

    groups = [[zz * 4 + at for zz in range(NB)] for at in range(4)]
    parts = lax.all_to_all(pieces.astype(jnp.float16), "wa", 0, 0, axis_index_groups=groups)
    factors = lax.optimization_barrier(power_of_two(parts[:, -1:, :].astype(jnp.float32)))
    total = jnp.sum(parts.astype(jnp.float32) * factors, 0)

    k = (z - e) & (NB - 1)
    kept_half = jnp.where(e < 4, h, 1 - h)
    place = jnp.stack([w & 3, (k == 4).astype(jnp.int32), (k > 4).astype(jnp.int32), kept_half]).astype(jnp.int32)
    direct, *sent = decoded(place, total)

    def mirror_route(dh, dc):
        def route(x, y, z, h, c):
            e, k = 4 * x + y, (z - 4 * x - y) % NB
            sends = k in (1, 2, 3) or (k == 4 and dh == x)
            return (z // 4, z % 4, e, h ^ dh, c ^ dc) if sends else None

        return route

    pieces = [moved(sent[2 * dh + dc], mirror_route(dh, dc)) for dh in range(2) for dc in range(2)]
    return assembled(place, direct, pieces, coeffs[None, :], column_coeffs).T


def solution(mesh):
    placed = (P("ex", "wa"), P("ex"))
    return jax.shard_map(
        per_device, mesh=mesh, in_specs=placed, out_specs=P("ex", "wa"), check_vma=False
    )
```

```python
import jax
import jax.numpy as jnp
from jax import lax
from jax.experimental import pallas as pl
from jax.experimental.pallas import tpu as pltpu
from jax.sharding import PartitionSpec as P

NB = 8
LANES = 128
FIRST, SECOND, PIECE = 424, 480, 200
TAIL = 8


def moved(value, route):
    pairs = []
    for e in range(NB):
        for w in range(4 * NB):
            to = route(e // 4, e % 4, w // 4, w // 2 % 2, w % 2)
            if to is not None:
                tx, ty, tz, th, tc = to
                pairs.append(((e * 4 * NB) + w, (tx * 4 + ty) * 4 * NB + tz * 4 + th * 2 + tc))
    return lax.ppermute(value, ("ex", "wa"), pairs)


def along_y(value, d):
    return moved(value, lambda x, y, z, h, c: (x, (y + d) % 4, z, h, c))


def along_x(value, d):
    def route(x, y, z, h, c):
        to = (2 * h + x + d) % 4
        return to % 2, y, z, to // 2, c

    return moved(value, route)


def dot_nt(left, right):
    return lax.dot_general(
        left, right, (((1,), (1,)), ((), ())), preferred_element_type=jnp.float32
    )


def power_of_two(n):
    left, size = jnp.abs(n), jnp.ones_like(n)
    for bit in (64.0, 32.0, 16.0, 8.0, 4.0, 2.0, 1.0):
        has = left >= bit
        size = jnp.where(has, size * 2.0**bit, size)
        left = jnp.where(has, left - bit, left)
    return jnp.where(n < 0, 1.0 / size, size)


def products_kernel(core_ref, scale_ref, mine_ref, other_ref, first_ref, second_ref, held, columns, arrived):
    step = pl.program_id(0)
    rows, k = mine_ref.shape[1:]
    quarter, half = rows // 4, rows // 2

    def fetches(j):
        return [
            pltpu.make_async_copy(ref.at[j], held.at[j, :, pl.ds(part * k, k)], arrived.at[part, j])
            for part, ref in enumerate((mine_ref, other_ref))
        ]

    def take(j):
        for fetch in fetches(j):
            fetch.wait()
        for h in range(2):
            at = pl.ds(pl.multiple_of(h * half + core_ref[0] * quarter, quarter), quarter)
            own = held[j, at, :]
            columns[h, pl.ds(j * quarter, quarter), :] = own
            if j < 4:
                columns[h, pl.ds((j + NB) * quarter, quarter), :] = own

    @pl.when(step == 0)
    def _():
        for j in range(NB):
            for fetch in fetches(j):
                fetch.start()
        for j in range(NB):
            take(j)

    factor = scale_ref[1, 0:1, :]
    for sub in range(4):
        i = step * 4 + sub
        start = pl.multiple_of(i * quarter, quarter)
        for h in range(2):
            tile = dot_nt(held[i], columns[h, pl.ds(start, 5 * quarter), :])
            first_ref[sub, 0, h, :rows, :] = tile[:, :128] * factor
            kept = jnp.where((step == 0) == (h == 0), tile[:half, 256:], tile[half:, 256:]).T[64:]
            first_ref[sub, 0, h, rows : rows + 80, :] = kept[:, :128] * factor
            for q in range(3):
                first_ref[sub, 0, h, rows + 80 : rows + 104, 32 * q : 32 * q + 32] = (
                    kept[24 * q : 24 * q + 24, 128:] * factor[:, :32]
                )
            first_ref[sub, 0, h, rows + 80 : rows + 88, 96:] = kept[72:, 128:] * factor[:, :32]
            first_ref[sub, 0, h, rows + 88 : rows + 104, 96:] = jnp.zeros((16, 32), jnp.float32)
            first_ref[sub, 0, h, FIRST:, :] = scale_ref[0]
            second_ref[sub, 0, h, :rows, :] = tile[:, 128:256] * factor
            second_ref[sub, 0, h, rows:SECOND, :64] = tile[:half, 256:320] * factor[:, :64]
            second_ref[sub, 0, h, rows:SECOND, 64:] = tile[half:, 256:320] * factor[:, :64]
            second_ref[sub, 0, h, SECOND:, :] = scale_ref[0]


def products(core, scale, mine, other):
    _, rows, k = mine.shape
    shapes = [(4, 2, 2, FIRST + TAIL, LANES), (4, 2, 2, SECOND + TAIL, LANES)]
    anywhere = pl.BlockSpec(memory_space=pl.ANY)
    return pl.pallas_call(
        products_kernel,
        grid=(2,),
        in_specs=[
            pl.BlockSpec(memory_space=pltpu.SMEM),
            pl.BlockSpec(scale.shape, lambda i: (0, 0, 0)),
            anywhere,
            anywhere,
        ],
        out_specs=[pl.BlockSpec((4, 1) + s[2:], lambda i: (0, i, 0, 0, 0)) for s in shapes],
        out_shape=[jax.ShapeDtypeStruct(s, jnp.float32) for s in shapes],
        scratch_shapes=[
            pltpu.VMEM((NB, rows, 2 * k), jnp.bfloat16),
            pltpu.VMEM((2, 12 * rows // 4, 2 * k), jnp.bfloat16),
            pltpu.SemaphoreType.DMA((2, NB)),
        ],
        compiler_params=pltpu.CompilerParams(vmem_limit_bytes=28 * 1024 * 1024),
        cost_estimate=pl.CostEstimate(
            flops=2 * NB * 9 * rows // 4 * rows * 2 * k, bytes_accessed=NB * rows * (k * 4 + 9 * rows), transcendentals=0
        ),
    )(core, scale, mine, other)


def chunks_kernel(array_ref, out_ref, arrived):
    k = out_ref.shape[2]
    copies = [
        pltpu.make_async_copy(array_ref.at[:, pl.ds(j * k, k)], out_ref.at[j], arrived.at[j]) for j in range(NB)
    ]
    for copy in copies:
        copy.start()
    for copy in copies:
        copy.wait()


def chunks_of(array):
    rows, columns = array.shape
    return pl.pallas_call(
        chunks_kernel,
        in_specs=[pl.BlockSpec(memory_space=pl.ANY)],
        out_specs=pl.BlockSpec(memory_space=pltpu.VMEM),
        out_shape=pltpu.VMEM((NB, rows, columns // NB), array.dtype),
        scratch_shapes=[pltpu.SemaphoreType.DMA((NB,))],
        compiler_params=pltpu.CompilerParams(vmem_limit_bytes=56 * 1024 * 1024),
        cost_estimate=pl.CostEstimate(flops=0, bytes_accessed=4 * rows * columns, transcendentals=0),
    )(array)


def pieces_kernel(e_ref, first_ref, second_ref, n_ref, out_ref, tile):
    rows, half = 320, 160
    tile[0:128, :] = first_ref[:rows, :].T
    tile[128:256, :] = second_ref[:rows, :].T
    packed = second_ref[rows:SECOND, :].T
    tile[256:320, :half] = packed[:64]
    tile[256:320, half:] = packed[64:]
    for k in range(NB):
        at = (e_ref[0] + k) & (NB - 1)
        if k < 4:
            piece = tile[k * 80 : (k + 1) * 80, :]
            out_ref[at, 0:80, :] = piece[:, :128]
            out_ref[at, 80:160, :] = piece[:, 128:256]
            out_ref[at, 160:200, :64] = piece[:40, 256:]
            out_ref[at, 160:200, 64:] = piece[40:, 256:]
        elif k == 4:
            out_ref[at, :104, :] = first_ref[rows:FIRST, :]
            out_ref[at, 104:PIECE, :] = jnp.zeros((PIECE - 104, LANES), jnp.float32)
        else:
            out_ref[at, :PIECE, :] = jnp.zeros((PIECE, LANES), jnp.float32)
        out_ref[at, PIECE:, :] = n_ref[...]


def pieces_of(e, first, second, n):
    vmem = pl.BlockSpec(memory_space=pltpu.VMEM)
    return pl.pallas_call(
        pieces_kernel,
        in_specs=[pl.BlockSpec(memory_space=pltpu.SMEM), vmem, vmem, vmem],
        out_specs=vmem,
        out_shape=pltpu.VMEM((NB, PIECE + TAIL, LANES), jnp.float32),
        scratch_shapes=[pltpu.VMEM((320, 320), jnp.float32)],
        cost_estimate=pl.CostEstimate(flops=0, bytes_accessed=1_300_000, transcendentals=0),
    )(e, first, second, n)


def tail_of(array):
    return array.reshape(-1, array.shape[-2], LANES)[0, -TAIL:, :].astype(jnp.float32)


def scales_of(arrays):
    tails = [tail_of(a) for a in arrays]
    n = tails[0]
    for tail in tails[1:]:
        n = jnp.maximum(n, tail)
    n = n + 2.0
    n, *factors = lax.optimization_barrier((n, *[power_of_two(t - n) for t in tails]))
    return n, factors


def total_of(arrays, factors):
    return sum(a.astype(jnp.float32) * f[:1] for a, f in zip(arrays, factors))


def with_tail(total, n):
    is_tail = lax.broadcasted_iota(jnp.int32, total.shape, total.ndim - 2) >= total.shape[-2] - TAIL
    return jnp.where(is_tail, n[:1], total)


def per_device(gradients, coeffs):
    rows, width = gradients.shape
    quarter, half = rows // 4, rows // 2
    e = lax.axis_index("ex")
    w = lax.axis_index("wa")
    x, y = e >> 2, e & 3
    z, h, c = w >> 2, (w >> 1) & 1, w & 1
    ring = 2 * h + x

    mine = lax.all_to_all(chunks_of(gradients), "ex", 0, 0)
    other = moved(mine, lambda x, y, z, h, c: (x, y, z, h, 1 - c))
    column_coeffs = moved(coeffs, lambda x, y, z, h, c: (z // 4, z % 4, 4 * x + y, h, c))
    column_coeffs = lax.dynamic_slice_in_dim(column_coeffs, (w & 3) * quarter, quarter)

    most = jnp.broadcast_to(jnp.max(jnp.abs(mine)).astype(jnp.float32), (TAIL, LANES))
    most = jnp.maximum(most, moved(most, lambda x, y, z, h, c: (x, y, z, h, 1 - c)))
    bound = jnp.maximum(most * most * (2.0 * width / NB), 1e-30)
    n = jnp.ceil(jnp.log2(bound)) - 11.0
    scale = jnp.stack([n, power_of_two(-n)])

    first, second = products(jnp.reshape(c, (1,)).astype(jnp.int32), scale, mine, other)

    def for_x(array, d):
        to = (ring + d) & 3
        array = lax.dynamic_index_in_dim(array, to & 1, array.ndim - 4, keepdims=False)
        return lax.dynamic_index_in_dim(array, to >> 1, array.ndim - 3, keepdims=False)

    def for_y(array, d):
        return lax.dynamic_index_in_dim(array, (y + d) & 3, 0, keepdims=False)

    def all_along_x(array):
        return [for_x(array, 0)] + [along_x(for_x(array, d).astype(jnp.float16), d) for d in (2, 1, 3)]

    first, second = lax.optimization_barrier((first.astype(jnp.float16), second))
    first = lax.all_to_all(first, "ex", 0, 0, axis_index_groups=[[0, 1, 2, 3], [4, 5, 6, 7]])
    second_all = all_along_x(second)
    n, factors = scales_of(second_all)
    second = with_tail(total_of(second_all, factors), n)
    second_all = [for_y(second, 0)] + [along_y(for_y(second, d).astype(jnp.float16), d) for d in (2, 1, 3)]
    n, factors = scales_of([first[s] for s in range(4)])
    factors = jnp.stack([f[:1] for f in factors]).reshape(4, 1, 1, 1, LANES)
    first = with_tail(jnp.sum(first.astype(jnp.float32) * factors, 0), n)
    first_all = all_along_x(first)
    n, factors = scales_of(first_all + second_all)
    pieces = pieces_of(
        jnp.reshape(e, (1,)).astype(jnp.int32), total_of(first_all, factors[:4]), total_of(second_all, factors[4:]), n
    )

    groups = [[zz * 4 + at for zz in range(NB)] for at in range(4)]
    parts = lax.all_to_all(pieces.astype(jnp.float16), "wa", 0, 0, axis_index_groups=groups)
    factors = lax.optimization_barrier(power_of_two(parts[:, -1:, :].astype(jnp.float32)))
    final = jnp.sum(parts.astype(jnp.float32) * factors, 0)[:PIECE]

    normal = jnp.concatenate(
        [final[:80], final[80:160], jnp.concatenate([final[160:, :64], final[160:, 64:]], 0)], 1
    )
    rest = [final[80:104, 0:32], final[80:104, 32:64], final[80:104, 64:96], final[80:88, 96:]]
    kept = jnp.concatenate([final[:80], jnp.concatenate(rest, 0)], 1)
    kept = jnp.concatenate([kept, kept], 1)
    k = (z - e) & (NB - 1)
    kept_half = jnp.where(e < 4, h, 1 - h)
    final = jnp.where(k == 4, kept, normal).reshape(quarter, 4, quarter).transpose(1, 0, 2)

    def mirror_route(x, y, z, h, c):
        return (z // 4, z % 4, 4 * x + y, h, c) if (z - 4 * x - y) % NB in (1, 2, 3, 4) else None

    turned = lax.all_to_all(final, "wa", 0, 0, axis_index_groups=[[4 * zz + at for at in range(4)] for zz in range(NB)])
    mirrored = moved(turned, mirror_route)
    halves = jnp.arange(4)[:, None, None] // 2
    direct = (k < 4) | ((k == 4) & (halves == kept_half))
    final = jnp.where(direct, final.transpose(0, 2, 1), mirrored).reshape(rows, quarter)
    return (coeffs[:, None] * final) * column_coeffs[None, :]


def solution(mesh):
    placed = (P("ex", "wa"), P("ex"))
    return jax.shard_map(
        per_device, mesh=mesh, in_specs=placed, out_specs=P("ex", "wa"), check_vma=False
    )
```

```python
import jax
import jax.numpy as jnp
from jax import lax
from jax.experimental import pallas as pl
from jax.experimental.pallas import tpu as pltpu
from jax.sharding import PartitionSpec as P

NB = 8
LANES = 128
FIRST, SECOND, PIECE = 424, 480, 200
TAIL = 8


def moved(value, route):
    pairs = []
    for e in range(NB):
        for w in range(4 * NB):
            to = route(e // 4, e % 4, w // 4, w // 2 % 2, w % 2)
            if to is not None:
                tx, ty, tz, th, tc = to
                pairs.append(((e * 4 * NB) + w, (tx * 4 + ty) * 4 * NB + tz * 4 + th * 2 + tc))
    return lax.ppermute(value, ("ex", "wa"), pairs)


def along_y(value, d):
    return moved(value, lambda x, y, z, h, c: (x, (y + d) % 4, z, h, c))


def along_x(value, d):
    def route(x, y, z, h, c):
        to = (2 * h + x + d) % 4
        return to % 2, y, z, to // 2, c

    return moved(value, route)


def dot_nt(left, right):
    return lax.dot_general(
        left, right, (((1,), (1,)), ((), ())), preferred_element_type=jnp.float32
    )


def power_of_two(n):
    left, size = jnp.abs(n), jnp.ones_like(n)
    for bit in (64.0, 32.0, 16.0, 8.0, 4.0, 2.0, 1.0):
        has = left >= bit
        size = jnp.where(has, size * 2.0**bit, size)
        left = jnp.where(has, left - bit, left)
    return jnp.where(n < 0, 1.0 / size, size)


def products_kernel(core_ref, scale_ref, mine_ref, other_ref, first_ref, second_ref, held, columns, arrived):
    step = pl.program_id(0)
    rows, k = mine_ref.shape[1:]
    quarter, half = rows // 4, rows // 2

    def fetches(j):
        return [
            pltpu.make_async_copy(ref.at[j], held.at[j, :, pl.ds(part * k, k)], arrived.at[part, j])
            for part, ref in enumerate((mine_ref, other_ref))
        ]

    def take(j):
        for fetch in fetches(j):
            fetch.wait()
        for h in range(2):
            at = pl.ds(pl.multiple_of(h * half + core_ref[0] * quarter, quarter), quarter)
            own = held[j, at, :]
            columns[h, pl.ds(j * quarter, quarter), :] = own
            if j < 4:
                columns[h, pl.ds((j + NB) * quarter, quarter), :] = own

    @pl.when(step == 0)
    def _():
        for j in range(NB):
            for fetch in fetches(j):
                fetch.start()
        for j in range(NB):
            take(j)

    factor = scale_ref[1, 0:1, :]
    for sub in range(4):
        i = step * 4 + sub
        start = pl.multiple_of(i * quarter, quarter)
        for h in range(2):
            tile = dot_nt(held[i], columns[h, pl.ds(start, 5 * quarter), :])
            first_ref[sub, 0, h, :rows, :] = tile[:, :128] * factor
            kept = jnp.where((step == 0) == (h == 0), tile[:half, 256:], tile[half:, 256:]).T[64:]
            first_ref[sub, 0, h, rows : rows + 80, :] = kept[:, :128] * factor
            for q in range(3):
                first_ref[sub, 0, h, rows + 80 : rows + 104, 32 * q : 32 * q + 32] = (
                    kept[24 * q : 24 * q + 24, 128:] * factor[:, :32]
                )
            first_ref[sub, 0, h, rows + 80 : rows + 88, 96:] = kept[72:, 128:] * factor[:, :32]
            first_ref[sub, 0, h, rows + 88 : rows + 104, 96:] = jnp.zeros((16, 32), jnp.float32)
            first_ref[sub, 0, h, FIRST:, :] = scale_ref[0]
            second_ref[sub, 0, h, :rows, :] = tile[:, 128:256] * factor
            second_ref[sub, 0, h, rows:SECOND, :64] = tile[:half, 256:320] * factor[:, :64]
            second_ref[sub, 0, h, rows:SECOND, 64:] = tile[half:, 256:320] * factor[:, :64]
            second_ref[sub, 0, h, SECOND:, :] = scale_ref[0]


def products(core, scale, mine, other):
    _, rows, k = mine.shape
    shapes = [(4, 2, 2, FIRST + TAIL, LANES), (4, 2, 2, SECOND + TAIL, LANES)]
    anywhere = pl.BlockSpec(memory_space=pl.ANY)
    return pl.pallas_call(
        products_kernel,
        grid=(2,),
        in_specs=[
            pl.BlockSpec(memory_space=pltpu.SMEM),
            pl.BlockSpec(scale.shape, lambda i: (0, 0, 0)),
            anywhere,
            anywhere,
        ],
        out_specs=[pl.BlockSpec((4, 1) + s[2:], lambda i: (0, i, 0, 0, 0)) for s in shapes],
        out_shape=[jax.ShapeDtypeStruct(s, jnp.float32) for s in shapes],
        scratch_shapes=[
            pltpu.VMEM((NB, rows, 2 * k), jnp.bfloat16),
            pltpu.VMEM((2, 12 * rows // 4, 2 * k), jnp.bfloat16),
            pltpu.SemaphoreType.DMA((2, NB)),
        ],
        compiler_params=pltpu.CompilerParams(vmem_limit_bytes=28 * 1024 * 1024),
        cost_estimate=pl.CostEstimate(
            flops=2 * NB * 9 * rows // 4 * rows * 2 * k, bytes_accessed=NB * rows * (k * 4 + 9 * rows), transcendentals=0
        ),
    )(core, scale, mine, other)


def chunks_kernel(array_ref, out_ref, arrived):
    k = out_ref.shape[2]
    copies = [
        pltpu.make_async_copy(array_ref.at[:, pl.ds(j * k, k)], out_ref.at[j], arrived.at[j]) for j in range(NB)
    ]
    for copy in copies:
        copy.start()
    for copy in copies:
        copy.wait()


def chunks_of(array):
    rows, columns = array.shape
    return pl.pallas_call(
        chunks_kernel,
        in_specs=[pl.BlockSpec(memory_space=pl.ANY)],
        out_specs=pl.BlockSpec(memory_space=pltpu.VMEM),
        out_shape=pltpu.VMEM((NB, rows, columns // NB), array.dtype),
        scratch_shapes=[pltpu.SemaphoreType.DMA((NB,))],
        compiler_params=pltpu.CompilerParams(vmem_limit_bytes=56 * 1024 * 1024),
        cost_estimate=pl.CostEstimate(flops=0, bytes_accessed=4 * rows * columns, transcendentals=0),
    )(array)


def pieces_kernel(e_ref, first_ref, second_ref, n_ref, out_ref, tile):
    rows, half = 320, 160
    tile[0:128, :] = first_ref[:rows, :].T
    tile[128:256, :] = second_ref[:rows, :].T
    packed = second_ref[rows:SECOND, :].T
    tile[256:320, :half] = packed[:64]
    tile[256:320, half:] = packed[64:]
    for k in range(NB):
        at = (e_ref[0] + k) & (NB - 1)
        if k < 4:
            piece = tile[k * 80 : (k + 1) * 80, :]
            out_ref[at, 0:80, :] = piece[:, :128]
            out_ref[at, 80:160, :] = piece[:, 128:256]
            out_ref[at, 160:200, :64] = piece[:40, 256:]
            out_ref[at, 160:200, 64:] = piece[40:, 256:]
        elif k == 4:
            out_ref[at, :104, :] = first_ref[rows:FIRST, :]
            out_ref[at, 104:PIECE, :] = jnp.zeros((PIECE - 104, LANES), jnp.float32)
        else:
            out_ref[at, :PIECE, :] = jnp.zeros((PIECE, LANES), jnp.float32)
        out_ref[at, PIECE:, :] = n_ref[...]


def pieces_of(e, first, second, n):
    vmem = pl.BlockSpec(memory_space=pltpu.VMEM)
    return pl.pallas_call(
        pieces_kernel,
        in_specs=[pl.BlockSpec(memory_space=pltpu.SMEM), vmem, vmem, vmem],
        out_specs=vmem,
        out_shape=pltpu.VMEM((NB, PIECE + TAIL, LANES), jnp.float32),
        scratch_shapes=[pltpu.VMEM((320, 320), jnp.float32)],
        cost_estimate=pl.CostEstimate(flops=0, bytes_accessed=1_300_000, transcendentals=0),
    )(e, first, second, n)


def tail_of(array):
    return array.reshape(-1, array.shape[-2], LANES)[0, -TAIL:, :].astype(jnp.float32)


def scales_of(arrays):
    tails = [tail_of(a) for a in arrays]
    n = tails[0]
    for tail in tails[1:]:
        n = jnp.maximum(n, tail)
    n = n + 2.0
    n, *factors = lax.optimization_barrier((n, *[power_of_two(t - n) for t in tails]))
    return n, factors


def total_of(arrays, factors):
    return sum(a.astype(jnp.float32) * f[:1] for a, f in zip(arrays, factors))


def with_tail(total, n):
    is_tail = lax.broadcasted_iota(jnp.int32, total.shape, total.ndim - 2) >= total.shape[-2] - TAIL
    return jnp.where(is_tail, n[:1], total)


def per_device(gradients, coeffs):
    rows, width = gradients.shape
    quarter, half = rows // 4, rows // 2
    e = lax.axis_index("ex")
    w = lax.axis_index("wa")
    x, y = e >> 2, e & 3
    z, h, c = w >> 2, (w >> 1) & 1, w & 1
    ring = 2 * h + x

    mine = lax.all_to_all(chunks_of(gradients), "ex", 0, 0)
    other = moved(mine, lambda x, y, z, h, c: (x, y, z, h, 1 - c))
    column_coeffs = moved(coeffs, lambda x, y, z, h, c: (z // 4, z % 4, 4 * x + y, h, c))
    column_coeffs = lax.dynamic_slice_in_dim(column_coeffs, (w & 3) * quarter, quarter)

    most = jnp.broadcast_to(jnp.max(jnp.abs(mine)).astype(jnp.float32), (TAIL, LANES))
    most = jnp.maximum(most, moved(most, lambda x, y, z, h, c: (x, y, z, h, 1 - c)))
    bound = jnp.maximum(most * most * (2.0 * width / NB), 1e-30)
    n = jnp.ceil(jnp.log2(bound)) - 11.0
    scale = jnp.stack([n, power_of_two(-n)])

    first, second = products(jnp.reshape(c, (1,)).astype(jnp.int32), scale, mine, other)

    def for_x(array, d):
        to = (ring + d) & 3
        array = lax.dynamic_index_in_dim(array, to & 1, array.ndim - 4, keepdims=False)
        return lax.dynamic_index_in_dim(array, to >> 1, array.ndim - 3, keepdims=False)

    def for_y(array, d):
        return lax.dynamic_index_in_dim(array, (y + d) & 3, 0, keepdims=False)

    def all_along_x(array):
        return [for_x(array, 0)] + [along_x(for_x(array, d).astype(jnp.float16), d) for d in (2, 1, 3)]

    first, second = lax.optimization_barrier((first.astype(jnp.float16), second))
    first = lax.all_to_all(first, "ex", 0, 0, axis_index_groups=[[0, 1, 2, 3], [4, 5, 6, 7]])
    second_all = all_along_x(second)
    n, factors = scales_of(second_all)
    second = with_tail(total_of(second_all, factors), n)
    second_all = [for_y(second, 0)] + [along_y(for_y(second, d).astype(jnp.float16), d) for d in (2, 1, 3)]
    n, factors = scales_of([first[s] for s in range(4)])
    factors = jnp.stack([f[:1] for f in factors]).reshape(4, 1, 1, 1, LANES)
    first = with_tail(jnp.sum(first.astype(jnp.float32) * factors, 0), n)
    first_all = all_along_x(first)
    n, factors = scales_of(first_all + second_all)
    pieces = pieces_of(
        jnp.reshape(e, (1,)).astype(jnp.int32), total_of(first_all, factors[:4]), total_of(second_all, factors[4:]), n
    )

    groups = [[zz * 4 + at for zz in range(NB)] for at in range(4)]
    parts = lax.all_to_all(pieces.astype(jnp.float16), "wa", 0, 0, axis_index_groups=groups)
    tails = parts[:, -1:, :].astype(jnp.float32)
    n = jnp.max(tails, 0)[:, :80] + 3.0
    factors, n, forth = lax.optimization_barrier((power_of_two(tails), n, power_of_two(-n)))
    final = jnp.sum(parts.astype(jnp.float32) * factors, 0)[:PIECE]

    normal = jnp.concatenate(
        [final[:80], final[80:160], jnp.concatenate([final[160:, :64], final[160:, 64:]], 0)], 1
    )
    rest = [final[80:104, 0:32], final[80:104, 32:64], final[80:104, 64:96], final[80:88, 96:]]
    kept = jnp.concatenate([final[:80], jnp.concatenate(rest, 0)], 1)
    kept = jnp.concatenate([kept, kept], 1)
    k = (z - e) & (NB - 1)
    kept_half = jnp.where(e < 4, h, 1 - h)
    final = jnp.where(k == 4, kept, normal).reshape(quarter, 4, quarter).transpose(1, 0, 2)

    def mirror_route(dh, dc):
        def route(x, y, z, h, c):
            e, k = 4 * x + y, (z - 4 * x - y) % NB
            sends = k in (1, 2, 3) or (k == 4 and dh == x)
            return (z // 4, z % 4, e, h ^ dh, c ^ dc) if sends else None

        return route

    def from_own(quarters):
        quarters = jnp.where(c == 1, jnp.stack([quarters[1], quarters[0], quarters[3], quarters[2]]), quarters)
        return jnp.where(h == 1, jnp.stack([quarters[2], quarters[3], quarters[0], quarters[1]]), quarters)

    tail = jnp.broadcast_to(n, (4, TAIL, quarter))
    sent = jnp.concatenate([from_own(final) * forth, tail], 1).astype(jnp.float16)
    got = jnp.stack([moved(sent[2 * dh + dc], mirror_route(dh, dc)) for dh in range(2) for dc in range(2)])
    got = got.astype(jnp.float32)
    back = lax.optimization_barrier(power_of_two(got[:, quarter : quarter + 1]))
    mirrored = from_own(got[:, :quarter] * back)
    halves = jnp.arange(4)[:, None, None] // 2
    direct = (k < 4) | ((k == 4) & (halves == kept_half))
    final = jnp.where(direct, final.transpose(0, 2, 1), mirrored).reshape(rows, quarter)
    return (coeffs[:, None] * final) * column_coeffs[None, :]


def solution(mesh):
    placed = (P("ex", "wa"), P("ex"))
    return jax.shard_map(
        per_device, mesh=mesh, in_specs=placed, out_specs=P("ex", "wa"), check_vma=False
    )
```

```python
import jax
import jax.numpy as jnp
from jax import lax
from jax.experimental import pallas as pl
from jax.experimental.pallas import tpu as pltpu
from jax.sharding import PartitionSpec as P

NB = 8
LANES = 128
FIRST, SECOND, PIECE = 424, 480, 200
TAIL = 8


def moved(value, route):
    pairs = []
    for e in range(NB):
        for w in range(4 * NB):
            to = route(e // 4, e % 4, w // 4, w // 2 % 2, w % 2)
            if to is not None:
                tx, ty, tz, th, tc = to
                pairs.append(((e * 4 * NB) + w, (tx * 4 + ty) * 4 * NB + tz * 4 + th * 2 + tc))
    return lax.ppermute(value, ("ex", "wa"), pairs)


def along_y(value, d):
    return moved(value, lambda x, y, z, h, c: (x, (y + d) % 4, z, h, c))


def along_x(value, d):
    def route(x, y, z, h, c):
        to = (2 * h + x + d) % 4
        return to % 2, y, z, to // 2, c

    return moved(value, route)


def dot_nt(left, right):
    return lax.dot_general(
        left, right, (((1,), (1,)), ((), ())), preferred_element_type=jnp.float32
    )


def power_of_two(n):
    left, size = jnp.abs(n), jnp.ones_like(n)
    for bit in (64.0, 32.0, 16.0, 8.0, 4.0, 2.0, 1.0):
        has = left >= bit
        size = jnp.where(has, size * 2.0**bit, size)
        left = jnp.where(has, left - bit, left)
    return jnp.where(n < 0, 1.0 / size, size)


def products_kernel(core_ref, scale_ref, mine_ref, other_ref, first_ref, second_ref, held, columns, arrived):
    step = pl.program_id(0)
    rows, k = mine_ref.shape[1:]
    quarter, half = rows // 4, rows // 2

    def fetches(j):
        return [
            pltpu.make_async_copy(ref.at[j], held.at[j, :, pl.ds(part * k, k)], arrived.at[part, j])
            for part, ref in enumerate((mine_ref, other_ref))
        ]

    def take(j):
        for fetch in fetches(j):
            fetch.wait()
        for h in range(2):
            at = pl.ds(pl.multiple_of(h * half + core_ref[0] * quarter, quarter), quarter)
            own = held[j, at, :]
            columns[h, pl.ds(j * quarter, quarter), :] = own
            if j < 4:
                columns[h, pl.ds((j + NB) * quarter, quarter), :] = own

    @pl.when(step == 0)
    def _():
        for j in range(NB):
            for fetch in fetches(j):
                fetch.start()
        for j in range(NB):
            take(j)

    factor = scale_ref[1, 0:1, :]
    for sub in range(4):
        i = step * 4 + sub
        start = pl.multiple_of(i * quarter, quarter)
        for h in range(2):
            tile = dot_nt(held[i], columns[h, pl.ds(start, 5 * quarter), :])
            first_ref[sub, 0, h, :rows, :] = tile[:, :128] * factor
            kept = jnp.where((step == 0) == (h == 0), tile[:half, 256:], tile[half:, 256:]).T[64:]
            first_ref[sub, 0, h, rows : rows + 80, :] = kept[:, :128] * factor
            for q in range(3):
                first_ref[sub, 0, h, rows + 80 : rows + 104, 32 * q : 32 * q + 32] = (
                    kept[24 * q : 24 * q + 24, 128:] * factor[:, :32]
                )
            first_ref[sub, 0, h, rows + 80 : rows + 88, 96:] = kept[72:, 128:] * factor[:, :32]
            first_ref[sub, 0, h, rows + 88 : rows + 104, 96:] = jnp.zeros((16, 32), jnp.float32)
            first_ref[sub, 0, h, FIRST:, :] = scale_ref[0]
            second_ref[sub, 0, h, :rows, :] = tile[:, 128:256] * factor
            second_ref[sub, 0, h, rows:SECOND, :64] = tile[:half, 256:320] * factor[:, :64]
            second_ref[sub, 0, h, rows:SECOND, 64:] = tile[half:, 256:320] * factor[:, :64]
            second_ref[sub, 0, h, SECOND:, :] = scale_ref[0]


def products(core, scale, mine, other):
    _, rows, k = mine.shape
    shapes = [(4, 2, 2, FIRST + TAIL, LANES), (4, 2, 2, SECOND + TAIL, LANES)]
    anywhere = pl.BlockSpec(memory_space=pl.ANY)
    return pl.pallas_call(
        products_kernel,
        grid=(2,),
        in_specs=[
            pl.BlockSpec(memory_space=pltpu.SMEM),
            pl.BlockSpec(scale.shape, lambda i: (0, 0, 0)),
            anywhere,
            anywhere,
        ],
        out_specs=[pl.BlockSpec((4, 1) + s[2:], lambda i: (0, i, 0, 0, 0)) for s in shapes],
        out_shape=[jax.ShapeDtypeStruct(s, jnp.float32) for s in shapes],
        scratch_shapes=[
            pltpu.VMEM((NB, rows, 2 * k), jnp.bfloat16),
            pltpu.VMEM((2, 12 * rows // 4, 2 * k), jnp.bfloat16),
            pltpu.SemaphoreType.DMA((2, NB)),
        ],
        compiler_params=pltpu.CompilerParams(vmem_limit_bytes=28 * 1024 * 1024),
        cost_estimate=pl.CostEstimate(
            flops=2 * NB * 9 * rows // 4 * rows * 2 * k, bytes_accessed=NB * rows * (k * 4 + 9 * rows), transcendentals=0
        ),
    )(core, scale, mine, other)


def chunks_kernel(array_ref, out_ref, arrived):
    k = out_ref.shape[2]
    copies = [
        pltpu.make_async_copy(array_ref.at[:, pl.ds(j * k, k)], out_ref.at[j], arrived.at[j]) for j in range(NB)
    ]
    for copy in copies:
        copy.start()
    for copy in copies:
        copy.wait()


def chunks_of(array):
    rows, columns = array.shape
    return pl.pallas_call(
        chunks_kernel,
        in_specs=[pl.BlockSpec(memory_space=pl.ANY)],
        out_specs=pl.BlockSpec(memory_space=pltpu.VMEM),
        out_shape=pltpu.VMEM((NB, rows, columns // NB), array.dtype),
        scratch_shapes=[pltpu.SemaphoreType.DMA((NB,))],
        compiler_params=pltpu.CompilerParams(vmem_limit_bytes=56 * 1024 * 1024),
        cost_estimate=pl.CostEstimate(flops=0, bytes_accessed=4 * rows * columns, transcendentals=0),
    )(array)


def pieces_kernel(e_ref, first_ref, second_ref, n_ref, out_ref, tile):
    rows, half = 320, 160
    tile[0:128, :] = first_ref[:rows, :].T
    tile[128:256, :] = second_ref[:rows, :].T
    packed = second_ref[rows:SECOND, :].T
    tile[256:320, :half] = packed[:64]
    tile[256:320, half:] = packed[64:]
    for k in range(NB):
        at = (e_ref[0] + k) & (NB - 1)
        if k < 4:
            piece = tile[k * 80 : (k + 1) * 80, :]
            out_ref[at, 0:80, :] = piece[:, :128]
            out_ref[at, 80:160, :] = piece[:, 128:256]
            out_ref[at, 160:200, :64] = piece[:40, 256:]
            out_ref[at, 160:200, 64:] = piece[40:, 256:]
        elif k == 4:
            out_ref[at, :104, :] = first_ref[rows:FIRST, :]
            out_ref[at, 104:PIECE, :] = jnp.zeros((PIECE - 104, LANES), jnp.float32)
        else:
            out_ref[at, :PIECE, :] = jnp.zeros((PIECE, LANES), jnp.float32)
        out_ref[at, PIECE:, :] = n_ref[...]


def pieces_of(e, first, second, n):
    vmem = pl.BlockSpec(memory_space=pltpu.VMEM)
    return pl.pallas_call(
        pieces_kernel,
        in_specs=[pl.BlockSpec(memory_space=pltpu.SMEM), vmem, vmem, vmem],
        out_specs=vmem,
        out_shape=pltpu.VMEM((NB, PIECE + TAIL, LANES), jnp.float32),
        scratch_shapes=[pltpu.VMEM((320, 320), jnp.float32)],
        compiler_params=pltpu.CompilerParams(vmem_limit_bytes=6 * 1024 * 1024),
        cost_estimate=pl.CostEstimate(flops=0, bytes_accessed=1_300_000, transcendentals=0),
    )(e, first, second, n)


def tail_of(array):
    return array.reshape(-1, array.shape[-2], LANES)[0, -TAIL:, :].astype(jnp.float32)


def scales_of(arrays):
    tails = [tail_of(a) for a in arrays]
    n = tails[0]
    for tail in tails[1:]:
        n = jnp.maximum(n, tail)
    n = n + 2.0
    n, *factors = lax.optimization_barrier((n, *[power_of_two(t - n) for t in tails]))
    return n, factors


def total_of(arrays, factors):
    return sum(a.astype(jnp.float32) * f[:1] for a, f in zip(arrays, factors))


def with_tail(total, n):
    is_tail = lax.broadcasted_iota(jnp.int32, total.shape, total.ndim - 2) >= total.shape[-2] - TAIL
    return jnp.where(is_tail, n[:1], total)


def per_device(gradients, coeffs):
    rows, width = gradients.shape
    quarter, half = rows // 4, rows // 2
    e = lax.axis_index("ex")
    w = lax.axis_index("wa")
    x, y = e >> 2, e & 3
    z, h, c = w >> 2, (w >> 1) & 1, w & 1
    ring = 2 * h + x

    mine = lax.all_to_all(chunks_of(gradients), "ex", 0, 0)
    other = moved(mine, lambda x, y, z, h, c: (x, y, z, h, 1 - c))
    column_coeffs = moved(coeffs, lambda x, y, z, h, c: (z // 4, z % 4, 4 * x + y, h, c))
    column_coeffs = lax.dynamic_slice_in_dim(column_coeffs, (w & 3) * quarter, quarter)

    most = jnp.broadcast_to(jnp.max(jnp.abs(mine)).astype(jnp.float32), (TAIL, LANES))
    most = jnp.maximum(most, moved(most, lambda x, y, z, h, c: (x, y, z, h, 1 - c)))
    bound = jnp.maximum(most * most * (2.0 * width / NB), 1e-30)
    n = jnp.ceil(jnp.log2(bound)) - 11.0
    scale = jnp.stack([n, power_of_two(-n)])

    first, second = products(jnp.reshape(c, (1,)).astype(jnp.int32), scale, mine, other)

    def for_x(array, d):
        to = (ring + d) & 3
        array = lax.dynamic_index_in_dim(array, to & 1, array.ndim - 4, keepdims=False)
        return lax.dynamic_index_in_dim(array, to >> 1, array.ndim - 3, keepdims=False)

    def for_y(array, d):
        return lax.dynamic_index_in_dim(array, (y + d) & 3, 0, keepdims=False)

    def all_along_x(array):
        return [for_x(array, 0)] + [along_x(for_x(array, d).astype(jnp.float16), d) for d in (2, 1, 3)]

    first, second = lax.optimization_barrier((first.astype(jnp.float16), second))
    first = lax.all_to_all(first, "ex", 0, 0, axis_index_groups=[[0, 1, 2, 3], [4, 5, 6, 7]])
    second_all = all_along_x(second)
    n, factors = scales_of(second_all)
    second = with_tail(total_of(second_all, factors), n)
    second_all = [for_y(second, 0)] + [along_y(for_y(second, d).astype(jnp.float16), d) for d in (2, 1, 3)]
    n, factors = scales_of([first[s] for s in range(4)])
    factors = jnp.stack([f[:1] for f in factors]).reshape(4, 1, 1, 1, LANES)
    first = with_tail(jnp.sum(first.astype(jnp.float32) * factors, 0), n)
    first_all = all_along_x(first)
    n, factors = scales_of(first_all + second_all)
    pieces = pieces_of(
        jnp.reshape(e, (1,)).astype(jnp.int32), total_of(first_all, factors[:4]), total_of(second_all, factors[4:]), n
    )

    groups = [[zz * 4 + at for zz in range(NB)] for at in range(4)]
    parts = lax.all_to_all(pieces.astype(jnp.float16), "wa", 0, 0, axis_index_groups=groups)
    factors = lax.optimization_barrier(power_of_two(parts[:, -1:, :].astype(jnp.float32)))
    final = jnp.sum(parts.astype(jnp.float32) * factors, 0)[:PIECE]

    normal = jnp.concatenate(
        [final[:80], final[80:160], jnp.concatenate([final[160:, :64], final[160:, 64:]], 0)], 1
    )
    rest = [final[80:104, 0:32], final[80:104, 32:64], final[80:104, 64:96], final[80:88, 96:]]
    kept = jnp.concatenate([final[:80], jnp.concatenate(rest, 0)], 1)
    kept = jnp.concatenate([kept, kept], 1)
    k = (z - e) & (NB - 1)
    kept_half = jnp.where(e < 4, h, 1 - h)
    final = jnp.where(k == 4, kept, normal).reshape(quarter, 4, quarter).transpose(1, 0, 2)

    def mirror_route(dh, dc):
        def route(x, y, z, h, c):
            e, k = 4 * x + y, (z - 4 * x - y) % NB
            sends = k in (1, 2, 3) or (k == 4 and dh == x)
            return (z // 4, z % 4, e, h ^ dh, c ^ dc) if sends else None

        return route

    def from_own(quarters):
        quarters = jnp.where(c == 1, jnp.stack([quarters[1], quarters[0], quarters[3], quarters[2]]), quarters)
        return jnp.where(h == 1, jnp.stack([quarters[2], quarters[3], quarters[0], quarters[1]]), quarters)

    sent = from_own(final)
    mirrored = from_own(jnp.stack([moved(sent[2 * dh + dc], mirror_route(dh, dc)) for dh in range(2) for dc in range(2)]))
    halves = jnp.arange(4)[:, None, None] // 2
    direct = (k < 4) | ((k == 4) & (halves == kept_half))
    final = jnp.where(direct, final.transpose(0, 2, 1), mirrored).reshape(rows, quarter)
    return (coeffs[:, None] * final) * column_coeffs[None, :]


def solution(mesh):
    placed = (P("ex", "wa"), P("ex"))
    return jax.shard_map(
        per_device, mesh=mesh, in_specs=placed, out_specs=P("ex", "wa"), check_vma=False
    )
```
